512 devices in a mesh: group: 16 (over x, z_hi, core), seq: 32 (over z_lo, y).
Axes of the slice: x: 4, y: 4, z: 16 (z_hi: 2, z_lo: 8; z = z_hi * 8 + z_lo), core: 2. Of those that a mesh axis runs over, the one named last changes fastest.
Arguments:
- queries: bfloat16 [4, 32, 8192], P(None, 'group', 'seq'), may hold values from -128 to 128
- key_value_pages: bfloat16 [16, 512, 32, 2048], P('group', 'seq'), may hold values from -6 to 6
- key_value_scales: bfloat16 [16, 512, 16], P('group', 'seq'), may hold values from 0.5 to 2
- page_table: int32 [16, 32, 16], P('group', 'seq'), may hold values from 0 to 15, each once within a row
- context_len: int32 [32], P('group'), may hold values from 4 to 8192, as said below
- mig_dest: int32 [32, 256], P('group', 'seq'), may hold values from 0 to 15, as said below
Outputs:
- attended: bfloat16 [4, 32, 8192], P(None, 'group', 'seq')
- incoming_pages: bfloat16 [16, 512, 32, 2048], P('group', 'seq')
- incoming_scales: bfloat16 [16, 512, 16], P('group', 'seq')
The draws below stay inside these ranges and needn't reach their ends.
Inputs may be any that keep to these rules, and one draw needn't show every extreme that they name: `page_table`: each device's 16 entries name its pool slots, each once; slot q of a group uses entries q * 8 to (q + 1) * 8 - 1 for its local pages in order. `context_len`: the cached tokens of a request, the 4 newest included. `mig_dest`: entry s * 8 + j of request r names the group that receives the request's local page j on seq index s, or its home group r // 2 where the page stays. On each seq index a group sends at most one page to each other group.
All inputs are finite; a program needn't handle non-finite values.
Results may differ from the reference program's by a relative error of at most 0.0075.
Values may be sent and summed in bfloat16 or wider, within the bound.
A program may use at most 64 MiB of HBM per device.

```python
import math
import jax
import jax.numpy as jnp
from jax import lax

HQ = 64
KEY_HEADS = 8
HEAD_SIZE = 128
DECODE_STEPS = 4
RG = 2
PAGE_TOKENS = 32
PPR = 8
POOL_SLOTS = 16
LMAX = 8192
QUERY_PER_KEY = 8
ROWS = 32
N_GROUP = 16
N_SEQ = 32


def group_plan(key):
    ranking = jax.random.permutation(key, N_GROUP).astype(jnp.int32)
    busy_flags = ranking < N_GROUP // 2
    spare_groups = jnp.argsort(ranking)[N_GROUP // 2:].astype(jnp.int32)
    return (busy_flags, spare_groups)


def draw_queries(key, part):
    key = jax.random.fold_in(key, 5)
    key_one = jax.random.fold_in(key, 0)
    values = jnp.clip(jax.random.normal(key_one, (DECODE_STEPS, ROWS, HQ, HEAD_SIZE), jnp.float32), -6.0, 6.0)
    return values.reshape(DECODE_STEPS, ROWS, HQ * HEAD_SIZE).astype(jnp.bfloat16)


def draw_context_len(key, part):
    busy_flags, spare_groups = group_plan(key)
    key = jax.random.fold_in(key, 3)
    key_one, key_two = jax.random.split(key)
    longer = jax.random.randint(key_one, (ROWS,), LMAX // 2 + 1, LMAX + 1)
    shorter = jax.random.randint(key_two, (ROWS,), DECODE_STEPS, LMAX // 8 + 1)
    row_busy = jnp.repeat(busy_flags, RG)
    lengths = jnp.where(row_busy, longer, shorter)
    leader = jnp.argmax(busy_flags.astype(jnp.int32)).astype(jnp.int32) * RG
    return lengths.at[leader].set(LMAX).astype(jnp.int32)


def draw_mig_dest(key, part):
    busy_flags, spare_groups = group_plan(key)
    key = jax.random.fold_in(key, 7)
    key_one, key_two = jax.random.split(key)
    tail_pages = PPR - PPR // 2
    candidates = RG * tail_pages
    moving = min(N_GROUP // 2, candidates)
    device_keys = jax.random.split(key_one, N_GROUP * N_SEQ)
    ranking_tail = jax.vmap(lambda single_key: jax.random.permutation(single_key, candidates))(device_keys)
    ranking_tail = ranking_tail.reshape(N_GROUP, N_SEQ, RG, tail_pages).astype(jnp.int32)
    offsets = jax.random.randint(key_two, (N_GROUP, N_SEQ, 1, 1), 0, N_GROUP // 2)
    receivers = spare_groups[(ranking_tail + offsets) % (N_GROUP // 2)]
    home_ids = jnp.arange(N_GROUP, dtype=jnp.int32)[:, None, None, None]
    leaving = (ranking_tail < moving) & busy_flags[:, None, None, None]
    tail_dest = jnp.where(leaving, receivers, home_ids)
    head_dest = jnp.broadcast_to(home_ids, (N_GROUP, N_SEQ, RG, PPR // 2))
    whole = jnp.concatenate([head_dest, tail_dest], axis=3)
    return whole.transpose(0, 2, 1, 3).reshape(ROWS, N_SEQ * PPR).astype(jnp.int32)


def block_levels(key, dims, cuts, least, largest):
    gain = 1.0
    for dim, shards_of in cuts:
        heights = jax.random.uniform(jax.random.fold_in(jax.random.fold_in(key, 6), dim), (shards_of,), jnp.float32, least / len(cuts), largest / len(cuts))
        gain = gain * jnp.repeat(jnp.exp(heights), dims[dim] // shards_of).reshape((-1,) + (1,) * (len(dims) - 1 - dim))
    return gain


def gaussian(key, extent, width, reach, cuts=(), held_as=jnp.bfloat16):
    factor_of = block_levels(key, extent, cuts, -0.22, 0.18) if cuts else 1.0
    drawn = jax.random.normal(key, extent, jnp.float32) * width * factor_of
    return jnp.minimum(jnp.maximum(drawn, -reach), reach).astype(held_as)


def setup_inputs(seed: int = 0) -> dict:
    key_list = jax.random.split(jax.random.key(seed), 7)
    return {
        "queries": draw_queries(jax.random.fold_in(key_list[6], 71), 0),
        "key_value_pages": gaussian(key_list[1], (N_GROUP, N_SEQ * POOL_SLOTS, PAGE_TOKENS, 2 * KEY_HEADS * HEAD_SIZE), 1.0, 6.0, ((0, 16), (1, 32))),
        "key_value_scales": jnp.clip(jnp.exp(math.log(2.0) - 1.3862944 * jax.random.uniform(key_list[2], (N_GROUP, N_SEQ * POOL_SLOTS, 2 * KEY_HEADS), jnp.float32) ** block_levels(key_list[2], (N_GROUP, N_SEQ * POOL_SLOTS, 2 * KEY_HEADS), ((0, 16), (1, 32)), -0.2, 0.2)), 0.5, 2.0).astype(jnp.bfloat16),
        "page_table": jax.vmap(lambda own: jax.random.permutation(own, POOL_SLOTS))(jax.random.split(key_list[3], N_GROUP * N_SEQ)).reshape((N_GROUP, N_SEQ, POOL_SLOTS)).astype(jnp.int32),
        "context_len": draw_context_len(jax.random.fold_in(key_list[6], 71), 0),
        "mig_dest": draw_mig_dest(jax.random.fold_in(key_list[6], 71), 0),
    }


NEGATIVE = -1.0e30


def row_attention(query_vector, row_page_list, row_scale_list, length):
    token_total = row_page_list.shape[0] * row_page_list.shape[1]
    key_tile = row_page_list[:, :, :KEY_HEADS * HEAD_SIZE].reshape(token_total, KEY_HEADS, HEAD_SIZE).astype(jnp.float32)
    value_tile = row_page_list[:, :, KEY_HEADS * HEAD_SIZE:].reshape(token_total, KEY_HEADS, HEAD_SIZE).astype(jnp.float32)
    key_dequant_scale = jnp.repeat(row_scale_list[:, :KEY_HEADS].astype(jnp.float32), PAGE_TOKENS, axis=0)
    value_dequant_scale = jnp.repeat(row_scale_list[:, KEY_HEADS:].astype(jnp.float32), PAGE_TOKENS, axis=0)
    grouped_query = query_vector.reshape(DECODE_STEPS, KEY_HEADS, QUERY_PER_KEY, HEAD_SIZE).astype(jnp.float32)
    raw_score = jnp.einsum("tkgd,lkd->tkgl", grouped_query, key_tile, precision=lax.Precision.HIGHEST)
    scores = raw_score * key_dequant_scale.T[None, :, None, :] * (HEAD_SIZE ** -0.5)
    position = jnp.arange(token_total, dtype=jnp.int32)
    limits = length - DECODE_STEPS + 1 + jnp.arange(DECODE_STEPS, dtype=jnp.int32)
    visible = (position[None, :] < limits[:, None])[:, None, None, :]
    highest = jnp.max(jnp.where(visible, scores, NEGATIVE), axis=-1, keepdims=True)
    exponent_terms = jnp.where(visible, jnp.exp(scores - highest), 0.0)
    totals = jnp.sum(exponent_terms, axis=-1)
    weights = (exponent_terms * value_dequant_scale.T[None, :, None, :]).astype(jnp.bfloat16)
    weights = lax.optimization_barrier(weights)
    context = jnp.einsum("tkgl,lkd->tkgd", weights.astype(jnp.float32), value_tile, precision=lax.Precision.HIGHEST)
    output = context / totals[..., None]
    return output.reshape(DECODE_STEPS, HQ * HEAD_SIZE).astype(jnp.bfloat16)


def reference(queries, key_value_pages, key_value_scales, page_table, context_len, mig_dest):
    page_ids = jnp.arange(PPR * N_SEQ, dtype=jnp.int32)
    shard_of = page_ids % N_SEQ
    local_of = page_ids // N_SEQ

    def one_row(row_id):
        home_group = row_id // RG
        row_slot = row_id % RG
        group_table = page_table[home_group]
        pool_slots = group_table[shard_of, row_slot * PPR + local_of]
        source = (shard_of * POOL_SLOTS + pool_slots).astype(jnp.int32)
        row_page_list = key_value_pages[home_group][source]
        row_scale_list = key_value_scales[home_group][source]
        return row_attention(queries[:, row_id], row_page_list, row_scale_list, context_len[row_id])

    attended = lax.map(one_row, jnp.arange(ROWS, dtype=jnp.int32)).transpose(1, 0, 2)

    rows_iota = jnp.arange(ROWS, dtype=jnp.int32)
    home_of = jnp.broadcast_to((rows_iota // RG)[:, None, None], (ROWS, N_SEQ, PPR))
    slot_of = (rows_iota % RG)[:, None, None]
    seq_of = jnp.broadcast_to(jnp.arange(N_SEQ, dtype=jnp.int32)[None, :, None], (ROWS, N_SEQ, PPR))
    page_of = jnp.arange(PPR, dtype=jnp.int32)[None, None, :]
    pool_slots = page_table[home_of, seq_of, slot_of * PPR + page_of]
    source = (seq_of * POOL_SLOTS + pool_slots).astype(jnp.int32)
    destination = mig_dest.reshape(ROWS, N_SEQ, PPR)
    target = jnp.where(destination != home_of, destination, N_GROUP).astype(jnp.int32)
    lookup = jnp.full((N_GROUP, N_SEQ, N_GROUP), -1, jnp.int32).at[target, seq_of, home_of].set(source, mode="drop")
    group_ids = jnp.arange(N_GROUP, dtype=jnp.int32)[None, :]

    def collect(column):
        present = column >= 0
        clipped = jnp.maximum(column, 0).astype(jnp.int32)
        page_rows = key_value_pages[group_ids, clipped]
        scales = key_value_scales[group_ids, clipped]
        return (jnp.where(present[:, :, None, None], page_rows, jnp.zeros((), page_rows.dtype)),
                jnp.where(present[:, :, None], scales, jnp.zeros((), scales.dtype)))

    incoming_pages, incoming_scales = lax.map(collect, lookup)
    return (attended,
            incoming_pages.reshape(N_GROUP, N_SEQ * N_GROUP, PAGE_TOKENS, 2 * KEY_HEADS * HEAD_SIZE),
            incoming_scales.reshape(N_GROUP, N_SEQ * N_GROUP, 2 * KEY_HEADS))
```

```python
import functools

import jax
import jax.numpy as jnp
from jax import lax
from jax.experimental import pallas as pl
from jax.experimental.pallas import tpu as pltpu
from jax.sharding import PartitionSpec as P

NEGATIVE = -1e30
MESH = pl.DeviceIdType.MESH
NX, NH, NC, NZ, NY = 4, 2, 2, 8, 4
NG = NX * NH * NC
STEPS, RG, PPR, SLOTS, TOKENS = 4, 2, 8, 16, 32
HEADS, DIM = 8, 128
WIDTH = 2 * HEADS * DIM
LOCAL = SLOTS * TOKENS
ROWS = 16


def join(parts):
    context = parts[..., :DIM]
    highest = parts[..., DIM : DIM + 1]
    totals = parts[..., DIM + 1 : DIM + 2]
    top = jnp.max(highest, axis=0)
    factor = jnp.exp(highest - top[None])
    return jnp.sum(context * factor, axis=0), top, jnp.sum(totals * factor, axis=0)


def with_stats(top, total):
    lane = lax.broadcasted_iota(jnp.int32, top.shape[:-1] + (DIM,), top.ndim - 1)
    return jnp.where(lane == 0, top, total)


def kernel(
    table, ctx, mig, query, scales, pages,
    att, out_pages, out_scales,
    pool, send, qall, part, yland, zpart, zland, scale_rows, sc_send, sc_recv,
    pool_sem, own_sem,
    zq_s, zq_r, yq_s, yq_r, pg_s, pg_r, sc_s, sc_r, yr_s, yr_r, zr_s, zr_r,
):
    g = lax.axis_index("group")
    s = lax.axis_index("seq")
    x, zh, c = g // (NH * NC), (g // NC) % NH, g % NC
    zl, y = s // NY, s % NY

    def along_z(d):
        return (g, lax.rem(zl + d, NZ) * NY + y)

    def along_y(d):
        return (g, zl * NY + lax.rem(y + d, NY))

    def along_group(d):
        dx, dc, dz = (d // NC) % NX, d % NC, 1 - d // (NX * NC)
        return (lax.rem(x + dx, NX) * NH + lax.rem(zh + dz, NH)) * NC + lax.rem(c + dc, NC)

    group_steps = [d for d in range(NG) if d != NX * NC]

    load_pool = pltpu.make_async_copy(pages, pool, pool_sem)
    load_pool.start()

    barrier = pltpu.get_barrier_semaphore()
    for d in group_steps:
        pl.semaphore_signal(barrier, 1, device_id=(along_group(d), s), device_id_type=MESH)
    for d in range(1, NZ):
        pl.semaphore_signal(barrier, 1, device_id=along_z(d), device_id_type=MESH)
    for d in range(1, NY):
        pl.semaphore_signal(barrier, 1, device_id=along_y(d), device_id_type=MESH)
    pl.semaphore_wait(barrier, NG - 1 + NZ - 1 + NY - 1)

    z_queries = []
    for d in range(1, NZ):
        copy = pltpu.make_async_remote_copy(
            query, qall.at[y, zl], zq_s.at[d], zq_r.at[d], device_id=along_z(d), device_id_type=MESH
        )
        copy.start()
        z_queries.append(copy)
    qall[y, zl] = query[...]

    load_pool.wait()

    def page_copy(d, h):
        return pltpu.make_async_remote_copy(
            send.at[h], out_pages.at[g], pg_s.at[d], pg_r.at[d], device_id=(h, s), device_id_type=MESH
        )

    def page_for(h):
        found = jnp.int32(0)
        slot = jnp.int32(0)
        for r in range(RG):
            for j in range(PPR):
                here = mig[r, j] == h
                slot = jnp.where(here, table[0, 0, r * PPR + j], slot)
                found = jnp.where(here, 1, found)
        return slot, found

    def send_page(i, carry):
        d = jnp.where(i < NX * NC, i, i + 1)
        h = along_group(d)
        slot, found = page_for(h)
        value = pool[slot]
        send[h] = jnp.where(found > 0, value, jnp.zeros_like(value))
        page_copy(d, h).start()
        return carry

    lax.fori_loop(0, NG - 1, send_page, 0)
    send[g] = jnp.zeros((TOKENS, WIDTH), jnp.bfloat16)
    own_page = pltpu.make_async_copy(send.at[g], out_pages.at[g], own_sem)
    own_page.start()

    slot_iota = lax.broadcasted_iota(jnp.int32, (NG, SLOTS), 1)
    dest_iota = lax.broadcasted_iota(jnp.int32, (NG, SLOTS), 0)
    chosen = jnp.zeros((NG, SLOTS), jnp.float32)
    token = lax.broadcasted_iota(jnp.int32, (8, LOCAL), 1)
    token_slot, token_in = token // TOKENS, token % TOKENS
    position = jnp.zeros((8, LOCAL), jnp.int32)
    owner = jnp.zeros((8, LOCAL), jnp.int32)
    for r in range(RG):
        for j in range(PPR):
            slot = table[0, 0, r * PPR + j]
            dest = mig[r, j]
            chosen = jnp.where(
                (dest_iota == dest) & (slot_iota == slot) & (dest_iota != g), 1.0, chosen
            )
            mine = token_slot == slot
            position = jnp.where(mine, (j * NZ * NY + s) * TOKENS + token_in, position)
            owner = jnp.where(mine, r, owner)
    own_scales = scales[...]
    rows = jnp.dot(chosen.astype(jnp.bfloat16), own_scales, preferred_element_type=jnp.float32)
    rows = jnp.concatenate([rows, jnp.zeros((NG, DIM - 2 * HEADS), jnp.float32)], axis=1)
    for h in range(NG):
        sc_send[h] = rows[h : h + 1]
    sc_recv[g] = jnp.zeros((1, DIM), jnp.float32)
    sc_copies = []
    for d in group_steps:
        h = along_group(d)
        copy = pltpu.make_async_remote_copy(
            sc_send.at[h], sc_recv.at[g], sc_s.at[d], sc_r.at[d], device_id=(h, s), device_id_type=MESH
        )
        copy.start()
        sc_copies.append(copy)

    for copy in z_queries:
        copy.wait()
    y_queries = []
    for d in range(1, NY):
        copy = pltpu.make_async_remote_copy(
            qall.at[y], qall.at[y], yq_s.at[d], yq_r.at[d], device_id=along_y(d), device_id_type=MESH
        )
        copy.start()
        y_queries.append(copy)

    spread = (
        lax.broadcasted_iota(jnp.int32, (SLOTS, LOCAL), 1) // TOKENS
        == lax.broadcasted_iota(jnp.int32, (SLOTS, LOCAL), 0)
    )
    scale_rows[...] = lax.dot_general(
        own_scales, jnp.where(spread, 1.0, 0.0).astype(jnp.bfloat16),
        (((0,), (0,)), ((), ())), preferred_element_type=jnp.float32,
    )
    row = lax.broadcasted_iota(jnp.int32, (NY * ROWS, LOCAL), 0)
    row_request, row_step = (row // 8) % RG, row % STEPS
    limit = jnp.where(row_request == 0, ctx[0], ctx[1]) - STEPS + 1 + row_step
    visible = (position[:1] < limit) & (owner[:1] == row_request)

    for copy in y_queries:
        copy.wait()

    for k in range(HEADS):
        query_rows = qall[:, k].reshape(NY * ROWS, DIM)
        keys = pool[:, :, k * DIM : (k + 1) * DIM].reshape(LOCAL, DIM)
        values = pool[:, :, (HEADS + k) * DIM : (HEADS + k + 1) * DIM].reshape(LOCAL, DIM)
        raw = lax.dot_general(
            query_rows, keys, (((1,), (1,)), ((), ())), preferred_element_type=jnp.float32
        )
        scores = raw * (scale_rows[k : k + 1, :] * DIM**-0.5)
        top = jnp.max(jnp.where(visible, scores, NEGATIVE), axis=1, keepdims=True)
        terms = jnp.where(visible, jnp.exp(scores - top), 0.0)
        total = jnp.sum(terms, axis=1, keepdims=True)
        weights = (terms * scale_rows[HEADS + k : HEADS + k + 1, :]).astype(jnp.bfloat16)
        context = jnp.dot(weights, values, preferred_element_type=jnp.float32)
        part[:, k, :, :DIM] = context.reshape(NY, ROWS, DIM)
        part[:, k, :, DIM:] = with_stats(top, total).reshape(NY, ROWS, DIM)

    y_parts = []
    for d in range(1, NY):
        to = lax.rem(y + d, NY)
        copy = pltpu.make_async_remote_copy(
            part.at[to], yland.at[y], yr_s.at[d], yr_r.at[d], device_id=along_y(d), device_id_type=MESH
        )
        copy.start()
        y_parts.append(copy)
    yland[y] = part[y]
    for copy in y_parts:
        copy.wait()
    for k in range(HEADS):
        context, top, total = join(yland[:, k])
        zpart[k, :, :DIM] = context
        zpart[k, :, DIM:] = with_stats(top, total)

    z_parts = []
    for d in range(1, NZ):
        to = lax.rem(zl + d, NZ)
        copy = pltpu.make_async_remote_copy(
            zpart.at[to], zland.at[zl], zr_s.at[d], zr_r.at[d], device_id=along_z(d), device_id_type=MESH
        )
        copy.start()
        z_parts.append(copy)
    zland[zl] = zpart[zl]
    for copy in z_parts:
        copy.wait()
    context, top, total = join(zland[...])
    att[...] = (context / total).astype(jnp.bfloat16)

    for copy in sc_copies:
        copy.wait()
    for h in range(NG):
        out_scales[h : h + 1, :] = sc_recv[h]

    def wait_page(i, carry):
        d = jnp.where(i < NX * NC, i, i + 1)
        page_copy(d, along_group(d)).wait()
        return carry

    lax.fori_loop(0, NG - 1, wait_page, 0)
    own_page.wait()


def local(queries, key_value_pages, key_value_scales, page_table, context_len, mig_dest):
    query = queries.reshape(STEPS, RG, 2, DIM).transpose(1, 2, 0, 3).reshape(ROWS, DIM)
    dma = pltpu.SemaphoreType.DMA
    vmem = pl.BlockSpec(memory_space=pltpu.VMEM)
    smem = pl.BlockSpec(memory_space=pltpu.SMEM)
    hbm = pl.BlockSpec(memory_space=pl.ANY)
    att, got_pages, got_scales = pl.pallas_call(
        kernel,
        out_shape=(
            jax.ShapeDtypeStruct((ROWS, DIM), jnp.bfloat16),
            jax.ShapeDtypeStruct((NG, TOKENS, WIDTH), jnp.bfloat16),
            jax.ShapeDtypeStruct((NG, DIM), jnp.float32),
        ),
        in_specs=[smem, smem, smem, vmem, vmem, hbm],
        out_specs=(vmem, hbm, vmem),
        scratch_shapes=[
            pltpu.VMEM((SLOTS, TOKENS, WIDTH), jnp.bfloat16),
            pltpu.VMEM((NG, TOKENS, WIDTH), jnp.bfloat16),
            pltpu.VMEM((NY, NZ, ROWS, DIM), jnp.bfloat16),
            pltpu.VMEM((NY, NZ, ROWS, 2 * DIM), jnp.float32),
            pltpu.VMEM((NY, NZ, ROWS, 2 * DIM), jnp.float32),
            pltpu.VMEM((NZ, ROWS, 2 * DIM), jnp.float32),
            pltpu.VMEM((NZ, ROWS, 2 * DIM), jnp.float32),
            pltpu.VMEM((2 * HEADS, LOCAL), jnp.float32),
            pltpu.VMEM((NG, 1, DIM), jnp.float32),
            pltpu.VMEM((NG, 1, DIM), jnp.float32),
            dma, dma,
            dma((NZ,)), dma((NZ,)), dma((NY,)), dma((NY,)),
            dma((NG,)), dma((NG,)), dma((NG,)), dma((NG,)),
            dma((NY,)), dma((NY,)), dma((NZ,)), dma((NZ,)),
        ],
        compiler_params=pltpu.CompilerParams(
            collective_id=0, has_side_effects=True, vmem_limit_bytes=40 * 2**20
        ),
        name="attend_and_migrate",
    )(page_table, context_len, mig_dest, query, key_value_scales[0], key_value_pages[0])
    attended = (
        att.reshape(RG, 2, STEPS, DIM).transpose(2, 0, 1, 3).reshape(STEPS, RG, 2 * DIM)
    )
    return attended, got_pages[None], got_scales[:, : 2 * HEADS].astype(jnp.bfloat16)[None]


def solution(mesh):
    return jax.shard_map(
        local,
        mesh=mesh,
        in_specs=(
            P(None, "group", "seq"),
            P("group", "seq", None, None),
            P("group", "seq", None),
            P("group", "seq", None),
            P("group"),
            P("group", "seq"),
        ),
        out_specs=(P(None, "group", "seq"), P("group", "seq", None, None), P("group", "seq", None)),
        check_vma=False,
    )
```

```python
import functools

import jax
import jax.numpy as jnp
from jax import lax
from jax.experimental import pallas as pl
from jax.experimental.pallas import tpu as pltpu
from jax.sharding import PartitionSpec as P

NEGATIVE = -1e30
MESH = pl.DeviceIdType.MESH
NX, NH, NC, NZ, NY = 4, 2, 2, 8, 4
NG = NX * NH * NC
COLS = NX * NC
STEPS, RG, PPR, SLOTS, TOKENS = 4, 2, 8, 16, 32
HEADS, DIM = 8, 128
WIDTH = 2 * HEADS * DIM
LOCAL = SLOTS * TOKENS
ROWS = 16
STRIPE = WIDTH // COLS
PARTS, PART_ROWS, PART_COLS = 4, 16, 128
PAIRS = COLS * COLS
ROOM = (16, 25, 36, PAIRS)


def join(parts):
    context = parts[..., :DIM]
    highest = parts[..., DIM : DIM + 1]
    totals = parts[..., DIM + 1 : DIM + 2]
    top = jnp.max(highest, axis=0)
    factor = jnp.exp(highest - top[None])
    return jnp.sum(context * factor, axis=0), top, jnp.sum(totals * factor, axis=0)


def with_stats(top, total):
    lane = lax.broadcasted_iota(jnp.int32, top.shape[:-1] + (DIM,), top.ndim - 1)
    return jnp.where(lane == 0, top, total)


def group_of(column, half):
    return ((column // NC) * NH + half) * NC + column % NC


class Place:
    def __init__(self):
        self.g = lax.axis_index("group")
        self.s = lax.axis_index("seq")
        self.x, self.zh, self.c = self.g // (NH * NC), (self.g // NC) % NH, self.g % NC
        self.zl, self.y = self.s // NY, self.s % NY
        self.column = self.x * NC + self.c

    def along_z(self, d):
        return (self.g, lax.rem(self.zl + d, NZ) * NY + self.y)

    def along_y(self, d):
        return (self.g, self.zl * NY + lax.rem(self.y + d, NY))

    def column_at(self, d):
        return lax.rem(self.x + d // NC, NX) * NC + lax.rem(self.c + d % NC, NC)


def remote(src, dst, send_sem, recv_sem, device):
    return pltpu.make_async_remote_copy(
        src, dst, send_sem, recv_sem, device_id=device, device_id_type=MESH
    )


def greet(devices):
    barrier = pltpu.get_barrier_semaphore()
    for device in devices:
        pl.semaphore_signal(barrier, 1, device_id=device, device_id_type=MESH)
    pl.semaphore_wait(barrier, len(devices))


def first_kernel(
    table_in, ctx_in, mig_in, query_in, scales_in, pages_in,
    packed_out, half_out, flags_out, count_out, zpart_out, scales_out,
    table, ctx, mig, query, scales, pool, half, stripes, relay, packed,
    qall, part, yland, scale_rows, sc_send, sc_recv, fl_send, fl_recv, flags,
    cz, cy, count, following, index,
    in_sem, out_sem,
    zq_s, zq_r, yq_s, yq_r, st_s, st_r, sc_s, sc_r, fl_s, fl_r, yr_s, yr_r, cz_s, cz_r, cy_s, cy_r,
):
    here = Place()
    g, s, zh, zl, y, column = here.g, here.s, here.zh, here.zl, here.y, here.column
    loads = [
        pltpu.make_async_copy(a, b, in_sem.at[i])
        for i, (a, b) in enumerate(
            [(mig_in, mig), (table_in, table), (query_in, query), (pages_in, pool), (scales_in, scales), (ctx_in, ctx)]
        )
    ]
    for copy in loads:
        copy.start()

    group_peers = [
        (group_of(here.column_at(d % COLS), lax.rem(zh + d // COLS, NH)), s) for d in range(1, NG)
    ]
    greet(
        group_peers
        + [here.along_z(d) for d in range(1, NZ)]
        + [here.along_y(d) for d in range(1, NY)]
    )

    for copy in loads[:3]:
        copy.wait()
    lane = lax.broadcasted_iota(jnp.int32, (1, DIM), 1)
    row_flags = jnp.zeros((1, DIM), jnp.int32)
    for r in range(RG):
        for j in range(PPR):
            row_flags = jnp.where((lane == mig[r, j]) & (lane != g), 1, row_flags)
    fl_send[...] = row_flags
    fl_recv[g] = row_flags
    flag_copies = []
    for d, peer in enumerate(group_peers, 1):
        copy = remote(fl_send, fl_recv.at[g], fl_s.at[d], fl_r.at[d], peer)
        copy.start()
        flag_copies.append(copy)

    z_queries = []
    for d in range(1, NZ):
        copy = remote(query, qall.at[y, zl], zq_s.at[d], zq_r.at[d], here.along_z(d))
        copy.start()
        z_queries.append(copy)
    qall[y, zl] = query[...]

    def page_for(h):
        found, slot = jnp.int32(0), jnp.int32(0)
        for r in range(RG):
            for j in range(PPR):
                mine = mig[r, j] == h
                slot = jnp.where(mine, table[0, 0, r * PPR + j], slot)
                found = jnp.where(mine, 1, found)
        return jnp.where(h == g, 0, found), slot

    loads[3].wait()

    def cut_page(b, carry):
        found, slot = page_for(group_of(b, 1 - zh))
        value = pool[slot]
        value = jnp.where(found > 0, value, jnp.zeros_like(value))
        for i in range(COLS):
            stripes[i, b] = value[:, i * STRIPE : (i + 1) * STRIPE]
        return carry

    lax.fori_loop(0, COLS, cut_page, 0)
    stripe_copies = []
    for d in range(1, COLS):
        i = here.column_at(d)
        copy = remote(
            stripes.at[i], relay.at[pl.ds(column * COLS, COLS)], st_s.at[d], st_r.at[d],
            (group_of(i, zh), s),
        )
        copy.start()
        stripe_copies.append(copy)
    relay[pl.ds(column * COLS, COLS)] = stripes[column]

    def half_page(b, carry):
        found, slot = page_for(group_of(b, zh))
        value = pool[slot]
        half[b] = jnp.where(found > 0, value, jnp.zeros_like(value))
        return carry

    lax.fori_loop(0, COLS, half_page, 0)
    half_copy = pltpu.make_async_copy(half, half_out, out_sem.at[0])
    half_copy.start()

    loads[4].wait()
    slot_iota = lax.broadcasted_iota(jnp.int32, (NG, SLOTS), 1)
    dest_iota = lax.broadcasted_iota(jnp.int32, (NG, SLOTS), 0)
    chosen = jnp.zeros((NG, SLOTS), jnp.float32)
    token = lax.broadcasted_iota(jnp.int32, (8, LOCAL), 1)
    token_slot, token_in = token // TOKENS, token % TOKENS
    position = jnp.zeros((8, LOCAL), jnp.int32)
    owner = jnp.zeros((8, LOCAL), jnp.int32)
    for r in range(RG):
        for j in range(PPR):
            slot = table[0, 0, r * PPR + j]
            chosen = jnp.where(
                (dest_iota == mig[r, j]) & (slot_iota == slot) & (dest_iota != g), 1.0, chosen
            )
            mine = token_slot == slot
            position = jnp.where(mine, (j * NZ * NY + s) * TOKENS + token_in, position)
            owner = jnp.where(mine, r, owner)
    own_scales = scales[...]
    rows = jnp.dot(chosen.astype(jnp.bfloat16), own_scales, preferred_element_type=jnp.float32)
    rows = jnp.concatenate([rows, jnp.zeros((NG, DIM - 2 * HEADS), jnp.float32)], axis=1)
    for h in range(NG):
        sc_send[h] = rows[h : h + 1]
    sc_recv[g] = jnp.zeros((1, DIM), jnp.float32)
    scale_copies = []
    for d, peer in enumerate(group_peers, 1):
        copy = remote(sc_send.at[peer[0]], sc_recv.at[g], sc_s.at[d], sc_r.at[d], peer)
        copy.start()
        scale_copies.append(copy)

    for copy in flag_copies:
        copy.wait()
    flag_copy = pltpu.make_async_copy(fl_recv, flags, out_sem.at[1])
    flag_copy.start()
    source = lax.broadcasted_iota(jnp.int32, (NG, 1, DIM), 0)
    dest = lax.broadcasted_iota(jnp.int32, (NG, 1, DIM), 2)
    source_half, dest_half = (source // NC) % NH, (dest // NC) % NH
    sent = fl_recv[...].astype(jnp.float32)
    crossing = jnp.where(source_half != dest_half, sent, 0.0)
    per_half = [
        jnp.sum(jnp.sum(jnp.where(source_half == h, crossing, 0.0), axis=0), axis=1, keepdims=True)
        for h in range(NH)
    ]
    count[...] = jnp.broadcast_to(jnp.maximum(per_half[0], per_half[1]), (1, DIM))
    z_counts = []
    for d in range(1, NZ):
        copy = remote(count, cz.at[zl], cz_s.at[d], cz_r.at[d], here.along_z(d))
        copy.start()
        z_counts.append(copy)
    cz[zl] = count[...]

    for copy in z_queries:
        copy.wait()
    y_queries = []
    for d in range(1, NY):
        copy = remote(qall.at[y], qall.at[y], yq_s.at[d], yq_r.at[d], here.along_y(d))
        copy.start()
        y_queries.append(copy)

    loads[5].wait()
    spread = (
        lax.broadcasted_iota(jnp.int32, (SLOTS, LOCAL), 1) // TOKENS
        == lax.broadcasted_iota(jnp.int32, (SLOTS, LOCAL), 0)
    )
    scale_rows[...] = lax.dot_general(
        own_scales, jnp.where(spread, 1.0, 0.0).astype(jnp.bfloat16),
        (((0,), (0,)), ((), ())), preferred_element_type=jnp.float32,
    )
    row = lax.broadcasted_iota(jnp.int32, (NY * ROWS, LOCAL), 0)
    row_request, row_step = (row // 8) % RG, row % STEPS
    limit = jnp.where(row_request == 0, ctx[0], ctx[1]) - STEPS + 1 + row_step
    visible = (position[:1] < limit) & (owner[:1] == row_request)

    flag_copy.wait()
    following[PAIRS] = PAIRS - 1

    def look_back(i, carry):
        pair = PAIRS - 1 - i
        present = flags[group_of(pair // COLS, zh), 0, group_of(pair % COLS, 1 - zh)]
        following[pair] = jnp.where(present > 0, pair, following[pair + 1])
        return carry

    lax.fori_loop(0, PAIRS, look_back, 0)

    def list_pairs(i, cursor):
        pair = following[cursor]
        index[i] = pair
        return jnp.minimum(pair + 1, PAIRS)

    lax.fori_loop(0, PAIRS, list_pairs, jnp.int32(0))

    for copy in z_counts:
        copy.wait()
    count[...] = jnp.max(cz[...], axis=0)
    y_counts = []
    for d in range(1, NY):
        copy = remote(count, cy.at[y], cy_s.at[d], cy_r.at[d], here.along_y(d))
        copy.start()
        y_counts.append(copy)
    cy[y] = count[...]

    for copy in y_queries:
        copy.wait()
    for k in range(HEADS):
        query_rows = qall[:, k].reshape(NY * ROWS, DIM)
        keys = pool[:, :, k * DIM : (k + 1) * DIM].reshape(LOCAL, DIM)
        values = pool[:, :, (HEADS + k) * DIM : (HEADS + k + 1) * DIM].reshape(LOCAL, DIM)
        raw = lax.dot_general(
            query_rows, keys, (((1,), (1,)), ((), ())), preferred_element_type=jnp.float32
        )
        scores = raw * (scale_rows[k : k + 1, :] * DIM**-0.5)
        top = jnp.max(jnp.where(visible, scores, NEGATIVE), axis=1, keepdims=True)
        terms = jnp.where(visible, jnp.exp(scores - top), 0.0)
        total = jnp.sum(terms, axis=1, keepdims=True)
        weights = (terms * scale_rows[HEADS + k : HEADS + k + 1, :]).astype(jnp.bfloat16)
        context = jnp.dot(weights, values, preferred_element_type=jnp.float32)
        part[:, k, :, :DIM] = context.reshape(NY, ROWS, DIM)
        part[:, k, :, DIM:] = with_stats(top, total).reshape(NY, ROWS, DIM)

    y_parts = []
    for d in range(1, NY):
        to = lax.rem(y + d, NY)
        copy = remote(part.at[to], yland.at[y], yr_s.at[d], yr_r.at[d], here.along_y(d))
        copy.start()
        y_parts.append(copy)
    yland[y] = part[y]

    for copy in stripe_copies:
        copy.wait()

    def pack(i, carry):
        stripe = relay[index[i]]
        for p in range(PARTS):
            r0, c0 = (p // 2) * PART_ROWS, (p % 2) * PART_COLS
            packed[p, i] = stripe[r0 : r0 + PART_ROWS, c0 : c0 + PART_COLS]
        return carry

    lax.fori_loop(0, PAIRS, pack, 0)
    packed_copy = pltpu.make_async_copy(packed, packed_out, out_sem.at[2])
    packed_copy.start()
    flags_out[...] = fl_recv[...]

    for copy in y_parts:
        copy.wait()
    for k in range(HEADS):
        context, top, total = join(yland[:, k])
        zpart_out[k, :, :DIM] = context
        zpart_out[k, :, DIM:] = with_stats(top, total)

    for copy in scale_copies:
        copy.wait()
    for h in range(NG):
        scales_out[h : h + 1, :] = sc_recv[h]
    for copy in y_counts:
        copy.wait()
    count_out[...] = jnp.max(cy[...], axis=0)
    half_copy.wait()
    packed_copy.wait()


def second_kernel(
    room, packed, half, flags_in, zpart,
    att, out_pages,
    flags, rank, crossed_0, crossed_1, crossed_2, crossed_3, handed, zland, flag_sem, own_sem,
    cr_s, cr_r, ha_s, ha_r, hd_s, hd_r, zr_s, zr_r,
):
    crossed = (crossed_0, crossed_1, crossed_2, crossed_3)
    here = Place()
    g, s, zh, zl, column = here.g, here.s, here.zh, here.zl, here.column
    flag_copy = pltpu.make_async_copy(flags_in, flags, flag_sem)
    flag_copy.start()
    partner = (group_of(column, 1 - zh), s)
    peers = [here.column_at(d) for d in range(1, COLS)]
    greet(
        [partner]
        + [(group_of(i, zh), s) for i in peers]
        + [here.along_z(d) for d in range(1, NZ)]
    )

    crossings = []
    for p in range(PARTS):
        copy = remote(
            packed.at[p, pl.ds(0, room)], crossed[p], cr_s.at[p], cr_r.at[p], partner
        )
        copy.start()
        crossings.append(copy)

    z_parts = []
    for d in range(1, NZ):
        to = lax.rem(zl + d, NZ)
        copy = remote(zpart.at[to], zland.at[zl], zr_s.at[d], zr_r.at[d], here.along_z(d))
        copy.start()
        z_parts.append(copy)
    zland[zl] = zpart[zl]

    halves = []
    for d, i in enumerate(peers, 1):
        copy = remote(
            half.at[i], out_pages.at[here.x, zh, here.c], ha_s.at[d], ha_r.at[d], (group_of(i, zh), s)
        )
        copy.start()
        halves.append(copy)
    own_half = pltpu.make_async_copy(half.at[column], out_pages.at[here.x, zh, here.c], own_sem.at[PARTS])
    own_half.start()

    flag_copy.wait()

    def count_up(pair, before):
        present = flags[group_of(pair // COLS, 1 - zh), 0, group_of(pair % COLS, zh)]
        rank[pair] = jnp.where(present > 0, before, -1)
        return before + present

    lax.fori_loop(0, PAIRS, count_up, jnp.int32(0))

    handing, own_parts = [], []
    for p in range(PARTS):
        if p == PARTS // 2:
            for copy in z_parts:
                copy.wait()
            context, top, total = join(zland[...])
            att[...] = (context / total).astype(jnp.bfloat16)
        crossings[p].wait()

        def unpack(pair, carry):
            at = rank[pair]
            value = crossed[p][jnp.clip(at, 0, room - 1)]
            value = jnp.where(at >= 0, value, jnp.zeros_like(value))
            handed[p, pair % COLS, pair // COLS // NC, pair // COLS % NC] = value
            return carry

        lax.fori_loop(0, PAIRS, unpack, 0)
        r0, c0 = (p // 2) * PART_ROWS, (p % 2) * PART_COLS
        columns = pl.ds(pl.multiple_of(column * STRIPE + c0, PART_COLS), PART_COLS)
        target = out_pages.at[:, 1 - zh, :, pl.ds(r0, PART_ROWS), columns]
        for d, i in enumerate(peers, 1):
            copy = remote(handed.at[p, i], target, hd_s.at[p, d], hd_r.at[p, d], (group_of(i, zh), s))
            copy.start()
            handing.append(copy)
        copy = pltpu.make_async_copy(handed.at[p, column], target, own_sem.at[p])
        copy.start()
        own_parts.append(copy)

    for copy in halves + handing + [own_half] + own_parts:
        copy.wait()


dma = pltpu.SemaphoreType.DMA
vmem = pl.BlockSpec(memory_space=pltpu.VMEM)
hbm = pl.BlockSpec(memory_space=pl.ANY)


def second(room, identity):
    return pl.pallas_call(
        functools.partial(second_kernel, room),
        out_shape=(
            jax.ShapeDtypeStruct((ROWS, DIM), jnp.bfloat16),
            jax.ShapeDtypeStruct((NX, NH, NC, TOKENS, WIDTH), jnp.bfloat16),
        ),
        in_specs=[hbm, hbm, hbm, vmem],
        out_specs=(vmem, hbm),
        scratch_shapes=[
            pltpu.SMEM((NG, 1, DIM), jnp.int32),
            pltpu.SMEM((PAIRS,), jnp.int32),
            *[pltpu.VMEM((room, PART_ROWS, PART_COLS), jnp.bfloat16)] * PARTS,
            pltpu.VMEM((PARTS, COLS, NX, NC, PART_ROWS, PART_COLS), jnp.bfloat16),
            pltpu.VMEM((NZ, ROWS, 2 * DIM), jnp.float32),
            dma, dma((PARTS + 1,)),
            dma((PARTS,)), dma((PARTS,)), dma((COLS,)), dma((COLS,)),
            dma((PARTS, COLS)), dma((PARTS, COLS)), dma((NZ,)), dma((NZ,)),
        ],
        compiler_params=pltpu.CompilerParams(
            collective_id=identity, has_side_effects=True, vmem_limit_bytes=40 * 2**20
        ),
        name=f"cross_{room}",
    )


def local(queries, key_value_pages, key_value_scales, page_table, context_len, mig_dest):
    query = queries.reshape(STEPS, RG, 2, DIM).transpose(1, 2, 0, 3).reshape(ROWS, DIM)
    f32, bf16, i32 = jnp.float32, jnp.bfloat16, jnp.int32
    packed, half, flags, count, zpart, got_scales = pl.pallas_call(
        first_kernel,
        out_shape=(
            jax.ShapeDtypeStruct((PARTS, PAIRS, PART_ROWS, PART_COLS), bf16),
            jax.ShapeDtypeStruct((COLS, TOKENS, WIDTH), bf16),
            jax.ShapeDtypeStruct((NG, 1, DIM), i32),
            jax.ShapeDtypeStruct((1, DIM), f32),
            jax.ShapeDtypeStruct((NZ, ROWS, 2 * DIM), f32),
            jax.ShapeDtypeStruct((NG, DIM), f32),
        ),
        in_specs=[hbm] * 6,
        out_specs=(hbm, hbm, vmem, vmem, vmem, vmem),
        scratch_shapes=[
            pltpu.SMEM(page_table.shape, i32),
            pltpu.SMEM(context_len.shape, i32),
            pltpu.SMEM(mig_dest.shape, i32),
            pltpu.VMEM((ROWS, DIM), bf16),
            pltpu.VMEM((SLOTS, 2 * HEADS), bf16),
            pltpu.VMEM((SLOTS, TOKENS, WIDTH), bf16),
            pltpu.VMEM((COLS, TOKENS, WIDTH), bf16),
            pltpu.VMEM((COLS, COLS, TOKENS, STRIPE), bf16),
            pltpu.VMEM((PAIRS, TOKENS, STRIPE), bf16),
            pltpu.VMEM((PARTS, PAIRS, PART_ROWS, PART_COLS), bf16),
            pltpu.VMEM((NY, NZ, ROWS, DIM), bf16),
            pltpu.VMEM((NY, NZ, ROWS, 2 * DIM), f32),
            pltpu.VMEM((NY, NZ, ROWS, 2 * DIM), f32),
            pltpu.VMEM((2 * HEADS, LOCAL), f32),
            pltpu.VMEM((NG, 1, DIM), f32),
            pltpu.VMEM((NG, 1, DIM), f32),
            pltpu.VMEM((1, DIM), i32),
            pltpu.VMEM((NG, 1, DIM), i32),
            pltpu.SMEM((NG, 1, DIM), i32),
            pltpu.VMEM((NZ, 1, DIM), f32),
            pltpu.VMEM((NY, 1, DIM), f32),
            pltpu.VMEM((1, DIM), f32),
            pltpu.SMEM((PAIRS + 1,), i32),
            pltpu.SMEM((PAIRS,), i32),
            dma((6,)), dma((3,)),
            dma((NZ,)), dma((NZ,)), dma((NY,)), dma((NY,)), dma((COLS,)), dma((COLS,)),
            dma((NG,)), dma((NG,)), dma((NG,)), dma((NG,)), dma((NY,)), dma((NY,)),
            dma((NZ,)), dma((NZ,)), dma((NY,)), dma((NY,)),
        ],
        compiler_params=pltpu.CompilerParams(
            collective_id=0, has_side_effects=True, vmem_limit_bytes=40 * 2**20
        ),
        name="attend_and_pack",
    )(page_table, context_len, mig_dest, query, key_value_scales[0], key_value_pages[0])
    most = count[0, 0]
    choice = sum((most > room).astype(i32) for room in ROOM[:-1])
    att, got_pages = lax.switch(
        choice, [second(room, 1 + i) for i, room in enumerate(ROOM)], packed, half, flags, zpart
    )
    attended = (
        att.reshape(RG, 2, STEPS, DIM).transpose(2, 0, 1, 3).reshape(STEPS, RG, 2 * DIM)
    )
    return (
        attended,
        got_pages.reshape(1, NG, TOKENS, WIDTH),
        got_scales[:, : 2 * HEADS].astype(bf16)[None],
    )


def solution(mesh):
    return jax.shard_map(
        local,
        mesh=mesh,
        in_specs=(
            P(None, "group", "seq"),
            P("group", "seq", None, None),
            P("group", "seq", None),
            P("group", "seq", None),
            P("group"),
            P("group", "seq"),
        ),
        out_specs=(P(None, "group", "seq"), P("group", "seq", None, None), P("group", "seq", None)),
        check_vma=False,
    )
```

```python
import functools

import jax
import jax.numpy as jnp
from jax import lax
from jax.experimental import pallas as pl
from jax.experimental.pallas import tpu as pltpu
from jax.sharding import PartitionSpec as P

NEGATIVE = -1e30
MESH = pl.DeviceIdType.MESH
NX, NH, NC, NZ, NY = 4, 2, 2, 8, 4
NG = NX * NH * NC
COLS = NX * NC
STEPS, RG, PPR, SLOTS, TOKENS = 4, 2, 8, 16, 32
HEADS, DIM = 8, 128
WIDTH = 2 * HEADS * DIM
LOCAL = SLOTS * TOKENS
ROWS = 16
STRIPE = WIDTH // COLS
PARTS, PART_ROWS, PART_COLS = 4, 16, 128
PAIRS = COLS * COLS
FIRST = 16
ROOM = (25, 36, PAIRS)


def part_offsets(p):
    return (p // 2) * PART_ROWS, (p % 2) * PART_COLS


def split(value):
    high = value.astype(jnp.bfloat16).astype(jnp.float32)
    middle = (value - high).astype(jnp.bfloat16).astype(jnp.float32)
    return high, middle, value - high - middle


def with_lanes(base, first, spacing, value):
    lane = lax.broadcasted_iota(jnp.int32, base.shape, 1)
    for i, term in enumerate(split(value)):
        base = jnp.where(lane == first + i * spacing, term, base)
    return base


def join(contexts, levels):
    top = jnp.max(levels, axis=0)
    factor = jnp.exp(levels - top[None])
    total = jnp.sum(factor, axis=0)
    context = jnp.sum(contexts.astype(jnp.float32) * factor, axis=0) / total
    return context, jnp.maximum(top + jnp.log(total), NEGATIVE)


def group_of(column, half):
    return ((column // NC) * NH + half) * NC + column % NC


class Place:
    def __init__(self):
        self.g = lax.axis_index("group")
        self.s = lax.axis_index("seq")
        self.x, self.zh, self.c = self.g // (NH * NC), (self.g // NC) % NH, self.g % NC
        self.zl, self.y = self.s // NY, self.s % NY
        self.column = self.x * NC + self.c

    def along_z(self, d):
        return (self.g, lax.rem(self.zl + d, NZ) * NY + self.y)

    def along_y(self, d):
        return (self.g, self.zl * NY + lax.rem(self.y + d, NY))

    def column_at(self, d):
        return lax.rem(self.x + d // NC, NX) * NC + lax.rem(self.c + d % NC, NC)


def remote(src, dst, send_sem, recv_sem, device):
    copy = pltpu.make_async_remote_copy(
        src, dst, send_sem, recv_sem, device_id=device, device_id_type=MESH
    )
    copy.start()
    return copy


def inside(src, dst, sem):
    copy = pltpu.make_async_copy(src, dst, sem)
    copy.start()
    return copy


def wait(copies):
    for copy in copies:
        copy.wait()


def greet(devices):
    barrier = pltpu.get_barrier_semaphore()
    for device in devices:
        pl.semaphore_signal(barrier, 1, device_id=device, device_id_type=MESH)
    pl.semaphore_wait(barrier, len(devices))


def rank_pairs(flags, source_half, dest_half, rank):
    def count_up(pair, before):
        present = flags[pair // COLS, 0, group_of(pair % COLS, dest_half)]
        rank[pair] = jnp.where(present > 0, before, -1)
        return before + present

    lax.fori_loop(0, PAIRS, count_up, jnp.int32(0))


def hand_over(here, p, handed, out_pages, send_sems, recv_sems, own_sem):
    r0, c0 = part_offsets(p)
    columns = pl.ds(pl.multiple_of(here.column * STRIPE + c0, PART_COLS), PART_COLS)
    target = out_pages.at[:, 1 - here.zh, :, pl.ds(r0, PART_ROWS), columns]
    copies = []
    for d in range(1, COLS):
        i = here.column_at(d)
        copies.append(
            remote(
                handed.at[p, i], target, send_sems.at[p, d], recv_sems.at[p, d],
                (group_of(i, here.zh), here.s),
            )
        )
    copies.append(inside(handed.at[p, here.column], target, own_sem.at[p]))
    return copies


def first_kernel(
    table_in, ctx_in, mig_in, query_in, scales_in, pages_in,
    att_out, out_pages, scales_out, packed_out, crossed_out, same_out, other_out, count_out,
    table, ctx, mig, query, scales, pool, half, stripes, packed, handed,
    relay_0, relay_1, relay_2, relay_3, crossed_0, crossed_1, crossed_2, crossed_3,
    qmine, qall, ypart, yland, zpart, zland, scale_rows, sc_send, sc_recv, sc_all,
    fl_send, fl_same, fl_other, same, other, cz, cy, count,
    slots, found, following, index, rank,
    in_sem, out_sem, own_sem,
    zq_s, zq_r, yq_s, yq_r, st_s, st_r, cr_s, cr_r, ha_s, ha_r, hd_s, hd_r,
    sc_s, sc_r, fl_s, fl_r, yr_s, yr_r, zr_s, zr_r, cz_s, cz_r, cy_s, cy_r,
):
    relays = (relay_0, relay_1, relay_2, relay_3)
    crossed = (crossed_0, crossed_1, crossed_2, crossed_3)
    here = Place()
    g, s, zh, zl, y, column = here.g, here.s, here.zh, here.zl, here.y, here.column
    get_mig, get_table, get_query, get_pool, get_scales, get_ctx = [
        inside(a, b, in_sem.at[i])
        for i, (a, b) in enumerate(
            [(mig_in, mig), (table_in, table), (query_in, query), (pages_in, pool), (scales_in, scales), (ctx_in, ctx)]
        )
    ]
    same_peers = [(group_of(here.column_at(d), zh), s) for d in range(1, COLS)]
    other_peers = [(group_of(here.column_at(d), 1 - zh), s) for d in range(COLS)]
    z_peers = [here.along_z(d) for d in range(1, NZ)]
    y_peers = [here.along_y(d) for d in range(1, NY)]
    greet(same_peers + other_peers + z_peers + y_peers)

    get_mig.wait()
    lane = lax.broadcasted_iota(jnp.int32, (1, DIM), 1)
    row_flags = jnp.zeros((1, DIM), jnp.int32)
    for r in range(RG):
        for j in range(PPR):
            row_flags = jnp.where((lane == mig[r, j]) & (lane != g), 1, row_flags)
    fl_send[...] = row_flags
    fl_same[column] = row_flags
    same_flags = [
        remote(fl_send, fl_same.at[column], fl_s.at[d], fl_r.at[d], peer)
        for d, peer in enumerate(same_peers, 1)
    ]
    other_flags = [
        remote(fl_send, fl_other.at[column], fl_s.at[COLS + d], fl_r.at[COLS + d], peer)
        for d, peer in enumerate(other_peers)
    ]

    get_query.wait()
    mine = query[...].astype(jnp.float32)
    mine = jnp.concatenate(
        [
            mine[t, r : r + 1, hh * DIM : (hh + 1) * DIM]
            for r in range(RG) for hh in range(2) for t in range(STEPS)
        ],
        axis=0,
    ).astype(jnp.bfloat16)
    qmine[...] = mine
    qall[y, zl] = mine
    z_queries = [
        remote(qmine, qall.at[y, zl], zq_s.at[d], zq_r.at[d], peer) for d, peer in enumerate(z_peers, 1)
    ]

    get_table.wait()

    def find_pages(i, carry):
        h = group_of(i % COLS, jnp.where(i < COLS, 1 - zh, zh))
        here_too, slot = jnp.int32(0), jnp.int32(0)
        for r in range(RG):
            for j in range(PPR):
                hit = mig[r, j] == h
                slot = jnp.where(hit, table[0, 0, r * PPR + j], slot)
                here_too = jnp.where(hit, 1, here_too)
        slots[i] = slot
        found[i] = jnp.where(h == g, 0, here_too)
        return carry

    lax.fori_loop(0, 2 * COLS, find_pages, 0)
    get_pool.wait()
    stripe_copies = []
    for p in range(PARTS):
        r0, c0 = part_offsets(p)

        def cut_page(b, carry):
            value = pool[slots[b], r0 : r0 + PART_ROWS]
            value = jnp.where(found[b] > 0, value, jnp.zeros_like(value))
            for i in range(COLS):
                start = i * STRIPE + c0
                stripes[p, i, b] = value[:, start : start + PART_COLS]
            return carry

        lax.fori_loop(0, COLS, cut_page, 0)
        place = relays[p].at[pl.ds(column * COLS, COLS)]
        stripe_copies.append(
            [
                remote(stripes.at[p, here.column_at(d)], place, st_s.at[p, d], st_r.at[p, d], peer)
                for d, peer in enumerate(same_peers, 1)
            ]
        )
        relays[p][pl.ds(column * COLS, COLS)] = stripes[p, column]

    wait(same_flags)
    inside(fl_same, same, out_sem.at[0]).wait()
    following[PAIRS] = PAIRS - 1

    def look_back(i, carry):
        pair = PAIRS - 1 - i
        present = same[pair // COLS, 0, group_of(pair % COLS, 1 - zh)]
        following[pair] = jnp.where(present > 0, pair, following[pair + 1])
        return carry

    lax.fori_loop(0, PAIRS, look_back, 0)

    def list_pairs(i, cursor):
        pair = following[cursor]
        index[i] = pair
        return jnp.minimum(pair + 1, PAIRS)

    lax.fori_loop(0, PAIRS, list_pairs, jnp.int32(0))

    def pack(p, start, stop):
        def step(i, carry):
            packed[p, i] = relays[p][index[i]]
            return carry

        lax.fori_loop(start, stop, step, 0)

    crossings, y_queries, z_counts = [], [], []
    for p in range(PARTS):
        wait(stripe_copies[p])
        pack(p, 0, FIRST)
        crossings.append(
            remote(packed.at[p, pl.ds(0, FIRST)], crossed[p], cr_s.at[p], cr_r.at[p], other_peers[0])
        )
        if p == 0:
            wait(z_queries)
            y_queries = [
                remote(qall.at[y], qall.at[y], yq_s.at[d], yq_r.at[d], peer)
                for d, peer in enumerate(y_peers, 1)
            ]
        if p == 1:
            wait(other_flags)
            source = lax.broadcasted_iota(jnp.int32, (COLS, 1, DIM), 2)
            dest_half = (source // NC) % NH
            per_half = [
                jnp.sum(
                    jnp.sum(jnp.where(dest_half != h, rows[...].astype(jnp.float32), 0.0), axis=0),
                    axis=1, keepdims=True,
                )
                for rows, h in ((fl_same, zh), (fl_other, 1 - zh))
            ]
            count[...] = jnp.broadcast_to(jnp.maximum(per_half[0], per_half[1]), (1, DIM))
            cz[zl] = count[...]
            z_counts = [
                remote(count, cz.at[zl], cz_s.at[d], cz_r.at[d], peer) for d, peer in enumerate(z_peers, 1)
            ]
    other_copy = inside(fl_other, other, out_sem.at[1])

    def half_page(b, carry):
        value = pool[slots[COLS + b]]
        half[b] = jnp.where(found[COLS + b] > 0, value, jnp.zeros_like(value))
        return carry

    lax.fori_loop(0, COLS, half_page, 0)
    own_place = out_pages.at[here.x, zh, here.c]
    halves = [
        remote(half.at[here.column_at(d)], own_place, ha_s.at[d], ha_r.at[d], peer)
        for d, peer in enumerate(same_peers, 1)
    ]
    halves.append(inside(half.at[column], own_place, out_sem.at[2]))

    get_scales.wait()
    get_ctx.wait()
    slot_iota = lax.broadcasted_iota(jnp.int32, (NG, SLOTS), 1)
    dest_iota = lax.broadcasted_iota(jnp.int32, (NG, SLOTS), 0)
    chosen = jnp.zeros((NG, SLOTS), jnp.float32)
    token = lax.broadcasted_iota(jnp.int32, (8, LOCAL), 1)
    token_slot, token_in = token // TOKENS, token % TOKENS
    position = jnp.zeros((8, LOCAL), jnp.int32)
    owner = jnp.zeros((8, LOCAL), jnp.int32)
    for r in range(RG):
        for j in range(PPR):
            slot = table[0, 0, r * PPR + j]
            chosen = jnp.where(
                (dest_iota == mig[r, j]) & (slot_iota == slot) & (dest_iota != g), 1.0, chosen
            )
            hit = token_slot == slot
            position = jnp.where(hit, (j * NZ * NY + s) * TOKENS + token_in, position)
            owner = jnp.where(hit, r, owner)
    own_scales = scales[...]
    rows = jnp.dot(chosen.astype(jnp.bfloat16), own_scales, preferred_element_type=jnp.float32)
    rows = jnp.concatenate([rows, jnp.zeros((NG, DIM - 2 * HEADS), jnp.float32)], axis=1)
    for h in range(NG):
        sc_send[h] = rows[h : h + 1]
    sc_recv[g] = jnp.zeros((1, DIM), jnp.float32)
    scale_copies = [
        remote(sc_send.at[peer[0]], sc_recv.at[g], sc_s.at[d], sc_r.at[d], peer)
        for d, peer in enumerate(other_peers + same_peers)
    ]
    spread = (
        lax.broadcasted_iota(jnp.int32, (SLOTS, LOCAL), 1) // TOKENS
        == lax.broadcasted_iota(jnp.int32, (SLOTS, LOCAL), 0)
    )
    scale_rows[...] = lax.dot_general(
        own_scales, jnp.where(spread, 1.0, 0.0).astype(jnp.bfloat16),
        (((0,), (0,)), ((), ())), preferred_element_type=jnp.float32,
    )
    row = lax.broadcasted_iota(jnp.int32, (NY * ROWS, LOCAL), 0)
    row_request, row_step = (row // 8) % RG, row % STEPS
    limit = jnp.where(row_request == 0, ctx[0], ctx[1]) - STEPS + 1 + row_step
    visible = (position[:1] < limit) & (owner[:1] == row_request)

    wait(y_queries)
    levels = jnp.zeros((NY * ROWS, DIM), jnp.float32)
    for k in range(HEADS):
        query_rows = qall[:, k].reshape(NY * ROWS, DIM)
        keys = pool[:, :, k * DIM : (k + 1) * DIM].reshape(LOCAL, DIM)
        values = pool[:, :, (HEADS + k) * DIM : (HEADS + k + 1) * DIM].reshape(LOCAL, DIM)
        raw = lax.dot_general(
            query_rows, keys, (((1,), (1,)), ((), ())), preferred_element_type=jnp.float32
        )
        scores = raw * (scale_rows[k : k + 1, :] * DIM**-0.5)
        top = jnp.max(jnp.where(visible, scores, NEGATIVE), axis=1, keepdims=True)
        terms = jnp.where(visible, jnp.exp(scores - top), 0.0)
        total = jnp.sum(terms, axis=1, keepdims=True)
        weights = (terms * scale_rows[HEADS + k : HEADS + k + 1, :]).astype(jnp.bfloat16)
        context = jnp.dot(weights, values, preferred_element_type=jnp.float32)
        some = total > 0.0
        total = jnp.where(some, total, 1.0)
        ypart[:, k] = (context / total).astype(jnp.bfloat16).reshape(NY, ROWS, DIM)
        levels = with_lanes(levels, k, HEADS, jnp.where(some, top + jnp.log(total), NEGATIVE))
    ypart[:, HEADS] = levels.astype(jnp.bfloat16).reshape(NY, ROWS, DIM)

    y_parts = [
        remote(ypart.at[lax.rem(y + d, NY)], yland.at[y], yr_s.at[d], yr_r.at[d], peer)
        for d, peer in enumerate(y_peers, 1)
    ]
    yland[y] = ypart[y]

    wait(z_counts)
    count[...] = jnp.max(cz[...], axis=0)
    cy[y] = count[...]
    y_counts = [
        remote(count, cy.at[y], cy_s.at[d], cy_r.at[d], peer) for d, peer in enumerate(y_peers, 1)
    ]

    for p in range(PARTS):
        pack(p, FIRST, PAIRS)
    outs = [inside(packed, packed_out, out_sem.at[3])]

    wait(y_parts)
    terms = yland[:, HEADS].astype(jnp.float32)
    for k in range(HEADS):
        level = sum(terms[:, :, k + i * HEADS : k + i * HEADS + 1] for i in range(3))
        context, level = join(yland[:, k], level)
        zpart[k, 0] = context.astype(jnp.bfloat16)
        zpart[k, 1] = with_lanes(jnp.zeros((ROWS, DIM), jnp.float32), 0, 1, level).astype(jnp.bfloat16)
    z_parts = [
        remote(zpart.at[lax.rem(zl + d, NZ)], zland.at[zl], zr_s.at[d], zr_r.at[d], peer)
        for d, peer in enumerate(z_peers, 1)
    ]
    zland[zl] = zpart[zl]

    other_copy.wait()
    rank_pairs(other, 1 - zh, zh, rank)
    handing = []
    for p in range(PARTS):
        crossings[p].wait()

        def unpack(pair, carry):
            at = rank[pair]
            value = crossed[p][jnp.clip(at, 0, FIRST - 1)]
            value = jnp.where((at >= 0) & (at < FIRST), value, jnp.zeros_like(value))
            handed[p, pair % COLS, pair // COLS // NC, pair // COLS % NC] = value
            return carry

        lax.fori_loop(0, PAIRS, unpack, 0)
        handing += hand_over(here, p, handed, out_pages, hd_s, hd_r, own_sem)
        outs.append(inside(crossed[p], crossed_out.at[p], out_sem.at[4 + p]))

    wait(z_parts)
    terms = zland[:, 1].astype(jnp.float32)
    context, _ = join(zland[:, 0], sum(terms[:, :, i : i + 1] for i in range(3)))
    for t in range(STEPS):
        att_out[t] = jnp.concatenate(
            [
                jnp.concatenate(
                    [
                        context[r * 8 + hh * STEPS + t : r * 8 + hh * STEPS + t + 1]
                        for hh in range(2)
                    ],
                    axis=1,
                )
                for r in range(RG)
            ],
            axis=0,
        ).astype(jnp.bfloat16)

    wait(scale_copies)
    for h in range(NG):
        sc_all[h : h + 1, :] = sc_recv[h]
    scales_out[...] = sc_all[:, : 2 * HEADS].astype(jnp.bfloat16)
    same_out[...] = fl_same[...]
    other_out[...] = fl_other[...]
    wait(y_counts)
    count_out[...] = jnp.max(cy[...], axis=0)
    wait(halves)
    wait(outs)
    wait(handing)


def second_kernel(
    room, packed, first_in, other_in, pages_before,
    out_pages,
    other, rank, first, rest_0, rest_1, rest_2, rest_3, handed, in_sem, own_sem,
    cr_s, cr_r, hd_s, hd_r,
):
    rest = (rest_0, rest_1, rest_2, rest_3)
    here = Place()
    get_other = inside(other_in, other, in_sem.at[0])
    get_first = inside(first_in, first, in_sem.at[1])
    partner = (group_of(here.column, 1 - here.zh), here.s)
    greet([partner] + [(group_of(here.column_at(d), here.zh), here.s) for d in range(1, COLS)])
    crossings = [
        remote(packed.at[p, pl.ds(FIRST, room - FIRST)], rest[p], cr_s.at[p], cr_r.at[p], partner)
        for p in range(PARTS)
    ]
    get_other.wait()
    rank_pairs(other, 1 - here.zh, here.zh, rank)
    get_first.wait()
    handing = []
    for p in range(PARTS):
        crossings[p].wait()

        def unpack(pair, carry):
            at = rank[pair]
            early = first[p, jnp.clip(at, 0, FIRST - 1)]
            late = rest[p][jnp.clip(at - FIRST, 0, room - FIRST - 1)]
            value = jnp.where(at < FIRST, early, late)
            value = jnp.where(at >= 0, value, jnp.zeros_like(value))
            handed[p, pair % COLS, pair // COLS // NC, pair // COLS % NC] = value
            return carry

        lax.fori_loop(0, PAIRS, unpack, 0)
        handing += hand_over(here, p, handed, out_pages, hd_s, hd_r, own_sem)
    wait(handing)


dma = pltpu.SemaphoreType.DMA
VMEM_BYTES = 63 * 2**20
f32, bf16, i32 = jnp.float32, jnp.bfloat16, jnp.int32
vmem = pl.BlockSpec(memory_space=pltpu.VMEM)
hbm = pl.BlockSpec(memory_space=pltpu.HBM)
PART = (PART_ROWS, PART_COLS)
PAGES = (NX, NH, NC, TOKENS, WIDTH)
HANDED = (PARTS, COLS, NX, NC) + PART


def second(room, identity):
    return pl.pallas_call(
        functools.partial(second_kernel, room),
        out_shape=jax.ShapeDtypeStruct(PAGES, bf16),
        in_specs=[hbm] * 4,
        out_specs=hbm,
        input_output_aliases={3: 0},
        scratch_shapes=[
            pltpu.SMEM((COLS, 1, DIM), i32),
            pltpu.SMEM((PAIRS,), i32),
            pltpu.VMEM((PARTS, FIRST) + PART, bf16),
            *[pltpu.VMEM((room - FIRST,) + PART, bf16)] * PARTS,
            pltpu.VMEM(HANDED, bf16),
            dma((2,)), dma((PARTS,)),
            dma((PARTS,)), dma((PARTS,)), dma((PARTS, COLS)), dma((PARTS, COLS)),
        ],
        compiler_params=pltpu.CompilerParams(
            collective_id=identity, has_side_effects=True, vmem_limit_bytes=VMEM_BYTES
        ),
        name=f"cross_{room}",
    )


def local(queries, key_value_pages, key_value_scales, page_table, context_len, mig_dest):
    att, got_pages, got_scales, packed, crossed, same, other, count = pl.pallas_call(
        first_kernel,
        out_shape=(
            jax.ShapeDtypeStruct(queries.shape, bf16),
            jax.ShapeDtypeStruct(PAGES, bf16),
            jax.ShapeDtypeStruct((NG, 2 * HEADS), bf16),
            jax.ShapeDtypeStruct((PARTS, PAIRS) + PART, bf16),
            jax.ShapeDtypeStruct((PARTS, FIRST) + PART, bf16),
            jax.ShapeDtypeStruct((COLS, 1, DIM), i32),
            jax.ShapeDtypeStruct((COLS, 1, DIM), i32),
            jax.ShapeDtypeStruct((1, DIM), f32),
        ),
        in_specs=[hbm] * 6,
        out_specs=(vmem, hbm, vmem, hbm, hbm, vmem, vmem, vmem),
        scratch_shapes=[
            pltpu.SMEM(page_table.shape, i32),
            pltpu.SMEM(context_len.shape, i32),
            pltpu.SMEM(mig_dest.shape, i32),
            pltpu.VMEM(queries.shape, bf16),
            pltpu.VMEM((SLOTS, 2 * HEADS), bf16),
            pltpu.VMEM((SLOTS, TOKENS, WIDTH), bf16),
            pltpu.VMEM((COLS, TOKENS, WIDTH), bf16),
            pltpu.VMEM((PARTS, COLS, COLS) + PART, bf16),
            pltpu.VMEM((PARTS, PAIRS) + PART, bf16),
            pltpu.VMEM(HANDED, bf16),
            *[pltpu.VMEM((PAIRS,) + PART, bf16)] * PARTS,
            *[pltpu.VMEM((FIRST,) + PART, bf16)] * PARTS,
            pltpu.VMEM((ROWS, DIM), bf16),
            pltpu.VMEM((NY, NZ, ROWS, DIM), bf16),
            pltpu.VMEM((NY, HEADS + 1, ROWS, DIM), bf16),
            pltpu.VMEM((NY, HEADS + 1, ROWS, DIM), bf16),
            pltpu.VMEM((NZ, 2, ROWS, DIM), bf16),
            pltpu.VMEM((NZ, 2, ROWS, DIM), bf16),
            pltpu.VMEM((2 * HEADS, LOCAL), f32),
            pltpu.VMEM((NG, 1, DIM), f32),
            pltpu.VMEM((NG, 1, DIM), f32),
            pltpu.VMEM((NG, DIM), f32),
            pltpu.VMEM((1, DIM), i32),
            pltpu.VMEM((COLS, 1, DIM), i32),
            pltpu.VMEM((COLS, 1, DIM), i32),
            pltpu.SMEM((COLS, 1, DIM), i32),
            pltpu.SMEM((COLS, 1, DIM), i32),
            pltpu.VMEM((NZ, 1, DIM), f32),
            pltpu.VMEM((NY, 1, DIM), f32),
            pltpu.VMEM((1, DIM), f32),
            pltpu.SMEM((2 * COLS,), i32),
            pltpu.SMEM((2 * COLS,), i32),
            pltpu.SMEM((PAIRS + 1,), i32),
            pltpu.SMEM((PAIRS,), i32),
            pltpu.SMEM((PAIRS,), i32),
            dma((6,)), dma((4 + PARTS,)), dma((PARTS,)),
            dma((NZ,)), dma((NZ,)), dma((NY,)), dma((NY,)),
            dma((PARTS, COLS)), dma((PARTS, COLS)), dma((PARTS,)), dma((PARTS,)),
            dma((COLS,)), dma((COLS,)), dma((PARTS, COLS)), dma((PARTS, COLS)),
            dma((NG,)), dma((NG,)), dma((NG,)), dma((NG,)),
            dma((NY,)), dma((NY,)), dma((NZ,)), dma((NZ,)),
            dma((NZ,)), dma((NZ,)), dma((NY,)), dma((NY,)),
        ],
        compiler_params=pltpu.CompilerParams(
            collective_id=0, has_side_effects=True, vmem_limit_bytes=VMEM_BYTES
        ),
        name="attend_and_migrate",
    )(page_table, context_len, mig_dest, queries, key_value_scales[0], key_value_pages[0])
    most = count[0, 0]
    choice = sum((most > room).astype(i32) for room in (FIRST,) + ROOM[:-1])
    got_pages = lax.switch(
        choice,
        [lambda packed, crossed, other, pages: pages]
        + [second(room, 1 + i) for i, room in enumerate(ROOM)],
        packed, crossed, other, got_pages,
    )
    return att, got_pages.reshape(1, NG, TOKENS, WIDTH), got_scales[None]


def solution(mesh):
    return jax.shard_map(
        local,
        mesh=mesh,
        in_specs=(
            P(None, "group", "seq"),
            P("group", "seq", None, None),
            P("group", "seq", None),
            P("group", "seq", None),
            P("group"),
            P("group", "seq"),
        ),
        out_specs=(P(None, "group", "seq"), P("group", "seq", None, None), P("group", "seq", None)),
        check_vma=False,
    )
```

```python
import functools

import jax
import jax.numpy as jnp
from jax import lax
from jax.experimental import pallas as pl
from jax.experimental.pallas import tpu as pltpu
from jax.sharding import PartitionSpec as P

NEGATIVE = -1e30
MESH = pl.DeviceIdType.MESH
NX, NH, NC, NZ, NY = 4, 2, 2, 8, 4
NG = NX * NH * NC
COLS = NX * NC
STEPS, RG, PPR, SLOTS, TOKENS = 4, 2, 8, 16, 32
HEADS, DIM = 8, 128
WIDTH = 2 * HEADS * DIM
LOCAL = SLOTS * TOKENS
ROWS = 16
STRIPE = WIDTH // COLS
PARTS, PART_ROWS, PART_COLS = 4, 16, 128
PAIRS = COLS * COLS
UNROLL = 8
CHUNKS = 8
FIRST = 25
ROOM = (36, PAIRS)


def part_offsets(p):
    return (p // 2) * PART_ROWS, (p % 2) * PART_COLS


def split(value):
    high = value.astype(jnp.bfloat16).astype(jnp.float32)
    middle = (value - high).astype(jnp.bfloat16).astype(jnp.float32)
    return high, middle, value - high - middle


def with_lanes(base, first, spacing, value):
    lane = lax.broadcasted_iota(jnp.int32, base.shape, 1)
    for i, term in enumerate(split(value)):
        base = jnp.where(lane == first + i * spacing, term, base)
    return base


def join(contexts, levels):
    top = jnp.max(levels, axis=0)
    factor = jnp.exp(levels - top[None])
    total = jnp.sum(factor, axis=0)
    context = jnp.sum(contexts.astype(jnp.float32) * factor, axis=0) / total
    return context, jnp.maximum(top + jnp.log(total), NEGATIVE)


def group_of(column, half):
    return ((column // NC) * NH + half) * NC + column % NC


class Place:
    def __init__(self):
        self.g = lax.axis_index("group")
        self.s = lax.axis_index("seq")
        self.x, self.zh, self.c = self.g // (NH * NC), (self.g // NC) % NH, self.g % NC
        self.zl, self.y = self.s // NY, self.s % NY
        self.column = self.x * NC + self.c

    def along_z(self, d):
        return (self.g, lax.rem(self.zl + d, NZ) * NY + self.y)

    def along_y(self, d):
        return (self.g, self.zl * NY + lax.rem(self.y + d, NY))

    def column_at(self, d):
        return lax.rem(self.x + d // NC, NX) * NC + lax.rem(self.c + d % NC, NC)


def remote(src, dst, send_sem, recv_sem, device):
    copy = pltpu.make_async_remote_copy(
        src, dst, send_sem, recv_sem, device_id=device, device_id_type=MESH
    )
    copy.start()
    return copy


def inside(src, dst, sem):
    copy = pltpu.make_async_copy(src, dst, sem)
    copy.start()
    return copy


def wait(copies):
    for copy in copies:
        copy.wait()


def greet(devices):
    barrier = pltpu.get_barrier_semaphore()
    for device in devices:
        pl.semaphore_signal(barrier, 1, device_id=device, device_id_type=MESH)
    return lambda: pl.semaphore_wait(barrier, len(devices))


def repeat(start, stop, step, carry=0):
    def steps(i, carry):
        for k in range(UNROLL):
            carry = step(start + i * UNROLL + k, carry)
        return carry

    rounds = (stop - start) // UNROLL
    carry = lax.fori_loop(0, rounds, steps, carry)
    return lax.fori_loop(start + rounds * UNROLL, stop, step, carry)


def rank_pairs(flags, source_half, dest_half, rank):
    def count_up(pair, before):
        present = flags[pair // COLS, 0, group_of(pair % COLS, dest_half)]
        rank[pair] = jnp.where(present > 0, before, -1)
        return before + present

    repeat(0, PAIRS, count_up, jnp.int32(0))


def hand_over(here, p, handed, out_pages, send_sems, recv_sems, own_sem):
    r0, c0 = part_offsets(p)
    columns = pl.ds(pl.multiple_of(here.column * STRIPE + c0, PART_COLS), PART_COLS)
    target = out_pages.at[:, 1 - here.zh, :, pl.ds(r0, PART_ROWS), columns]
    copies = []
    for d in range(1, COLS):
        i = here.column_at(d)
        copies.append(
            remote(
                handed.at[p, i], target, send_sems.at[p, d], recv_sems.at[p, d],
                (group_of(i, here.zh), here.s),
            )
        )
    copies.append(inside(handed.at[p, here.column], target, own_sem.at[p]))
    return copies


def first_kernel(
    table_in, ctx_in, mig_in, query_in, scales_in, pages_in,
    att_out, out_pages, scales_out, packed_out, crossed_out, other_out, choice_out,
    table, ctx, mig, query, scales, pool, half, stripes, packed, handed,
    relay_0, relay_1, relay_2, relay_3, crossed_0, crossed_1, crossed_2, crossed_3,
    qmine, qall, ypart, yland, zpart, zland, scale_rows, sc_send, sc_recv, sc_all,
    fl_send, fl_same, fl_other, same, other, cz, cy, count,
    slots, found, following, index, rank,
    in_sem, out_sem, own_sem,
    zq_s, zq_r, yq_s, yq_r, st_s, st_r, cr_s, cr_r, ha_s, ha_r, hd_s, hd_r,
    sc_s, sc_r, fl_s, fl_r, yr_s, yr_r, zr_s, zr_r, cz_s, cz_r, cy_s, cy_r,
):
    relays = (relay_0, relay_1, relay_2, relay_3)
    crossed = (crossed_0, crossed_1, crossed_2, crossed_3)
    here = Place()
    g, s, zh, zl, y, column = here.g, here.s, here.zh, here.zl, here.y, here.column
    get_mig, get_table, get_query, get_pool, get_scales, get_ctx = [
        inside(a, b, in_sem.at[i])
        for i, (a, b) in enumerate(
            [(mig_in, mig), (table_in, table), (query_in, query), (pages_in, pool), (scales_in, scales), (ctx_in, ctx)]
        )
    ]
    same_peers = [(group_of(here.column_at(d), zh), s) for d in range(1, COLS)]
    other_peers = [(group_of(here.column_at(d), 1 - zh), s) for d in range(COLS)]
    z_peers = [here.along_z(d) for d in range(1, NZ)]
    y_peers = [here.along_y(d) for d in range(1, NY)]
    all_here = greet(other_peers + z_peers + same_peers + y_peers)

    get_mig.wait()
    lane = lax.broadcasted_iota(jnp.int32, (1, DIM), 1)
    row_flags = jnp.zeros((1, DIM), jnp.int32)
    for r in range(RG):
        for j in range(PPR):
            row_flags = jnp.where((lane == mig[r, j]) & (lane != g), 1, row_flags)
    fl_send[...] = row_flags
    fl_same[column] = row_flags
    get_table.wait()

    def find_pages(i, carry):
        h = group_of(i % COLS, jnp.where(i < COLS, 1 - zh, zh))
        here_too, slot = jnp.int32(0), jnp.int32(0)
        for r in range(RG):
            for j in range(PPR):
                hit = mig[r, j] == h
                slot = jnp.where(hit, table[0, 0, r * PPR + j], slot)
                here_too = jnp.where(hit, 1, here_too)
        slots[i] = slot
        found[i] = jnp.where(h == g, 0, here_too)
        return carry

    repeat(0, COLS, find_pages)
    get_pool.wait()
    for p in range(PARTS):
        r0, c0 = part_offsets(p)

        def cut_page(b, carry):
            value = pool[slots[b], r0 : r0 + PART_ROWS]
            value = jnp.where(found[b] > 0, value, jnp.zeros_like(value))
            for i in range(COLS):
                start = i * STRIPE + c0
                stripes[p, i, b] = value[:, start : start + PART_COLS]
            return carry

        repeat(0, COLS, cut_page)
        relays[p][pl.ds(column * COLS, COLS)] = stripes[p, column]
    all_here()
    same_flags = [
        remote(fl_send, fl_same.at[column], fl_s.at[d], fl_r.at[d], peer)
        for d, peer in enumerate(same_peers, 1)
    ]
    stripe_copies = []
    for p in range(PARTS):
        place = relays[p].at[pl.ds(column * COLS, COLS)]
        stripe_copies.append(
            [
                remote(stripes.at[p, here.column_at(d)], place, st_s.at[p, d], st_r.at[p, d], peer)
                for d, peer in enumerate(same_peers, 1)
            ]
        )

    other_flags = [
        remote(fl_send, fl_other.at[column], fl_s.at[COLS + d], fl_r.at[COLS + d], peer)
        for d, peer in enumerate(other_peers)
    ]

    get_query.wait()
    mine = query[...].astype(jnp.float32)
    mine = jnp.concatenate(
        [
            mine[t, r : r + 1, hh * DIM : (hh + 1) * DIM]
            for r in range(RG) for hh in range(2) for t in range(STEPS)
        ],
        axis=0,
    ).astype(jnp.bfloat16)
    qmine[...] = mine
    qall[y, zl] = mine
    z_queries = [
        remote(qmine, qall.at[y, zl], zq_s.at[d], zq_r.at[d], peer) for d, peer in enumerate(z_peers, 1)
    ]

    wait(same_flags)
    inside(fl_same, same, out_sem.at[0]).wait()
    following[PAIRS] = PAIRS - 1

    def look_back(i, carry):
        pair = PAIRS - 1 - i
        present = same[pair // COLS, 0, group_of(pair % COLS, 1 - zh)]
        following[pair] = jnp.where(present > 0, pair, following[pair + 1])
        return carry

    repeat(0, PAIRS, look_back)

    def list_pairs(i, cursor):
        pair = following[cursor]
        index[i] = pair
        return jnp.minimum(pair + 1, PAIRS)

    cursor = repeat(0, FIRST, list_pairs, jnp.int32(0))

    def pack(p, start, stop):
        def step(i, carry):
            packed[p, i] = relays[p][index[i]]
            return carry

        repeat(start, stop, step)

    crossings, y_queries, z_counts = [], [], []
    for p in range(PARTS):
        wait(stripe_copies[p])
        pack(p, 0, FIRST)
        crossings.append(
            remote(packed.at[p, pl.ds(0, FIRST)], crossed[p], cr_s.at[p], cr_r.at[p], other_peers[0])
        )
        if p == 0:
            wait(z_queries)
            y_queries = [
                remote(qall.at[y], qall.at[y], yq_s.at[d], yq_r.at[d], peer)
                for d, peer in enumerate(y_peers, 1)
            ]
        if p == 1:
            wait(other_flags)
            source = lax.broadcasted_iota(jnp.int32, (COLS, 1, DIM), 2)
            dest_half = (source // NC) % NH
            per_half = [
                jnp.sum(
                    jnp.sum(jnp.where(dest_half != h, rows[...].astype(jnp.float32), 0.0), axis=0),
                    axis=1, keepdims=True,
                )
                for rows, h in ((fl_same, zh), (fl_other, 1 - zh))
            ]
            count[...] = jnp.broadcast_to(jnp.maximum(per_half[0], per_half[1]), (1, DIM))
            cz[zl] = count[...]
            z_counts = [
                remote(count, cz.at[zl], cz_s.at[d], cz_r.at[d], peer) for d, peer in enumerate(z_peers, 1)
            ]
    other_copy = inside(fl_other, other, out_sem.at[1])

    repeat(COLS, 2 * COLS, find_pages)
    def half_page(b, carry):
        value = pool[slots[COLS + b]]
        half[b] = jnp.where(found[COLS + b] > 0, value, jnp.zeros_like(value))
        return carry

    lax.fori_loop(0, COLS, half_page, 0)
    own_place = out_pages.at[here.x, zh, here.c]
    halves = [
        remote(half.at[here.column_at(d)], own_place, ha_s.at[d], ha_r.at[d], peer)
        for d, peer in enumerate(same_peers, 1)
    ]
    halves.append(inside(half.at[column], own_place, out_sem.at[2]))

    get_scales.wait()
    get_ctx.wait()
    slot_iota = lax.broadcasted_iota(jnp.int32, (NG, SLOTS), 1)
    dest_iota = lax.broadcasted_iota(jnp.int32, (NG, SLOTS), 0)
    chosen = jnp.zeros((NG, SLOTS), jnp.float32)
    token = lax.broadcasted_iota(jnp.int32, (8, LOCAL), 1)
    token_slot, token_in = token // TOKENS, token % TOKENS
    position = jnp.zeros((8, LOCAL), jnp.int32)
    owner = jnp.zeros((8, LOCAL), jnp.int32)
    for r in range(RG):
        for j in range(PPR):
            slot = table[0, 0, r * PPR + j]
            chosen = jnp.where(
                (dest_iota == mig[r, j]) & (slot_iota == slot) & (dest_iota != g), 1.0, chosen
            )
            hit = token_slot == slot
            position = jnp.where(hit, (j * NZ * NY + s) * TOKENS + token_in, position)
            owner = jnp.where(hit, r, owner)
    own_scales = scales[...]
    rows = jnp.dot(chosen.astype(jnp.bfloat16), own_scales, preferred_element_type=jnp.float32)
    rows = jnp.concatenate([rows, jnp.zeros((NG, DIM - 2 * HEADS), jnp.float32)], axis=1)
    for h in range(NG):
        sc_send[h] = rows[h : h + 1]
    sc_recv[g] = jnp.zeros((1, DIM), jnp.float32)
    scale_copies = [
        remote(sc_send.at[peer[0]], sc_recv.at[g], sc_s.at[d], sc_r.at[d], peer)
        for d, peer in enumerate(other_peers + same_peers)
    ]
    spread = (
        lax.broadcasted_iota(jnp.int32, (SLOTS, LOCAL), 1) // TOKENS
        == lax.broadcasted_iota(jnp.int32, (SLOTS, LOCAL), 0)
    )
    scale_rows[...] = lax.dot_general(
        own_scales, jnp.where(spread, 1.0, 0.0).astype(jnp.bfloat16),
        (((0,), (0,)), ((), ())), preferred_element_type=jnp.float32,
    )
    row = lax.broadcasted_iota(jnp.int32, (NY * ROWS, LOCAL), 0)
    row_request, row_step = (row // 8) % RG, row % STEPS
    limit = jnp.where(row_request == 0, ctx[0], ctx[1]) - STEPS + 1 + row_step
    visible = (position[:1] < limit) & (owner[:1] == row_request)

    wait(y_queries)
    levels = jnp.zeros((NY * ROWS, DIM), jnp.float32)
    for k in range(HEADS):
        query_rows = qall[:, k].reshape(NY * ROWS, DIM)
        keys = pool[:, :, k * DIM : (k + 1) * DIM].reshape(LOCAL, DIM)
        values = pool[:, :, (HEADS + k) * DIM : (HEADS + k + 1) * DIM].reshape(LOCAL, DIM)
        raw = lax.dot_general(
            query_rows, keys, (((1,), (1,)), ((), ())), preferred_element_type=jnp.float32
        )
        scores = raw * (scale_rows[k : k + 1, :] * DIM**-0.5)
        top = jnp.max(jnp.where(visible, scores, NEGATIVE), axis=1, keepdims=True)
        terms = jnp.where(visible, jnp.exp(scores - top), 0.0)
        total = jnp.sum(terms, axis=1, keepdims=True)
        weights = (terms * scale_rows[HEADS + k : HEADS + k + 1, :]).astype(jnp.bfloat16)
        context = jnp.dot(weights, values, preferred_element_type=jnp.float32)
        some = total > 0.0
        total = jnp.where(some, total, 1.0)
        ypart[:, k] = (context / total).astype(jnp.bfloat16).reshape(NY, ROWS, DIM)
        levels = with_lanes(levels, k, HEADS, jnp.where(some, top + jnp.log(total), NEGATIVE))
    ypart[:, HEADS] = levels.astype(jnp.bfloat16).reshape(NY, ROWS, DIM)

    y_parts = [
        remote(ypart.at[lax.rem(y + d, NY)], yland.at[y], yr_s.at[d], yr_r.at[d], peer)
        for d, peer in enumerate(y_peers, 1)
    ]
    yland[y] = ypart[y]

    wait(z_counts)
    count[...] = jnp.max(cz[...], axis=0)
    cy[y] = count[...]
    y_counts = [
        remote(count, cy.at[y], cy_s.at[d], cy_r.at[d], peer) for d, peer in enumerate(y_peers, 1)
    ]

    repeat(FIRST, PAIRS, list_pairs, cursor)
    for p in range(PARTS):
        pack(p, FIRST, PAIRS)
    outs = [inside(packed, packed_out, out_sem.at[3])]

    wait(y_parts)
    terms = yland[:, HEADS].astype(jnp.float32)
    for k in range(HEADS):
        level = sum(terms[:, :, k + i * HEADS : k + i * HEADS + 1] for i in range(3))
        context, level = join(yland[:, k], level)
        zpart[k, 0] = context.astype(jnp.bfloat16)
        zpart[k, 1] = with_lanes(jnp.zeros((ROWS, DIM), jnp.float32), 0, 1, level).astype(jnp.bfloat16)
    z_parts = [
        remote(zpart.at[lax.rem(zl + d, NZ)], zland.at[zl], zr_s.at[d], zr_r.at[d], peer)
        for d, peer in enumerate(z_peers, 1)
    ]
    zland[zl] = zpart[zl]

    other_copy.wait()
    rank_pairs(other, 1 - zh, zh, rank)
    handing = []
    for p in range(PARTS):
        crossings[p].wait()

        def unpack(pair, carry):
            at = rank[pair]
            value = crossed[p][jnp.clip(at, 0, FIRST - 1)]
            value = jnp.where((at >= 0) & (at < FIRST), value, jnp.zeros_like(value))
            handed[p, pair % COLS, pair // COLS // NC, pair // COLS % NC] = value
            return carry

        repeat(0, PAIRS, unpack)
        handing += hand_over(here, p, handed, out_pages, hd_s, hd_r, own_sem)
        outs.append(inside(crossed[p], crossed_out.at[p], out_sem.at[4 + p]))

    wait(z_parts)
    terms = zland[:, 1].astype(jnp.float32)
    context, _ = join(zland[:, 0], sum(terms[:, :, i : i + 1] for i in range(3)))
    for t in range(STEPS):
        att_out[t] = jnp.concatenate(
            [
                jnp.concatenate(
                    [
                        context[r * 8 + hh * STEPS + t : r * 8 + hh * STEPS + t + 1]
                        for hh in range(2)
                    ],
                    axis=1,
                )
                for r in range(RG)
            ],
            axis=0,
        ).astype(jnp.bfloat16)

    wait(scale_copies)
    for h in range(NG):
        sc_all[h : h + 1, :] = sc_recv[h]
    scales_out[...] = sc_all[:, : 2 * HEADS].astype(jnp.bfloat16)
    other_out[...] = fl_other[...]
    wait(y_counts)
    most = jnp.max(cy[...], axis=0)
    choice_out[...] = sum((most > room).astype(jnp.int32) for room in (FIRST,) + ROOM[:-1])
    wait(halves)
    wait(outs)
    wait(handing)


def second_kernel(
    room, packed, first_in, other_in, pages_before,
    out_pages,
    other, rank, first, rest_0, rest_1, rest_2, rest_3, handed, in_sem, own_sem,
    cr_s, cr_r, hd_s, hd_r,
):
    rest = (rest_0, rest_1, rest_2, rest_3)
    here = Place()
    get_other = inside(other_in, other, in_sem.at[0])
    get_first = inside(first_in, first, in_sem.at[1])
    partner = (group_of(here.column, 1 - here.zh), here.s)
    greet([partner] + [(group_of(here.column_at(d), here.zh), here.s) for d in range(1, COLS)])()
    crossings = [
        remote(packed.at[p, pl.ds(FIRST, room - FIRST)], rest[p], cr_s.at[p], cr_r.at[p], partner)
        for p in range(PARTS)
    ]
    get_other.wait()
    rank_pairs(other, 1 - here.zh, here.zh, rank)
    get_first.wait()
    handing = []
    for p in range(PARTS):
        crossings[p].wait()

        def unpack(pair, carry):
            at = rank[pair]
            early = first[p, jnp.clip(at, 0, FIRST - 1)]
            late = rest[p][jnp.clip(at - FIRST, 0, room - FIRST - 1)]
            value = jnp.where(at < FIRST, early, late)
            value = jnp.where(at >= 0, value, jnp.zeros_like(value))
            handed[p, pair % COLS, pair // COLS // NC, pair // COLS % NC] = value
            return carry

        repeat(0, PAIRS, unpack)
        handing += hand_over(here, p, handed, out_pages, hd_s, hd_r, own_sem)
    wait(handing)


def last_kernel(att, pages, scales, att_out, pages_out, scales_out, held, att_held, scales_held, sems, out_sems):
    rows = NG // CHUNKS
    moves = [
        (pages.at[pl.ds(i * rows, rows)], held.at[pl.ds(i * rows, rows)], pages_out.at[0, pl.ds(i * rows, rows)])
        for i in range(CHUNKS)
    ]
    moves += [(att, att_held, att_out), (scales, scales_held, scales_out.at[0])]
    reads = [inside(a, b, sems.at[i]) for i, (a, b, _) in enumerate(moves)]
    writes = []
    for i, (_, b, c) in enumerate(moves):
        reads[i].wait()
        writes.append(inside(b, c, out_sems.at[i]))
    wait(writes)


dma = pltpu.SemaphoreType.DMA
VMEM_BYTES = 63 * 2**20
f32, bf16, i32 = jnp.float32, jnp.bfloat16, jnp.int32
vmem = pl.BlockSpec(memory_space=pltpu.VMEM)
hbm = pl.BlockSpec(memory_space=pltpu.HBM)
PART = (PART_ROWS, PART_COLS)
PAGES = (NX, NH, NC, TOKENS, WIDTH)
HANDED = (PARTS, COLS, NX, NC) + PART


def second(room, identity):
    return pl.pallas_call(
        functools.partial(second_kernel, room),
        out_shape=jax.ShapeDtypeStruct(PAGES, bf16),
        in_specs=[hbm] * 4,
        out_specs=hbm,
        input_output_aliases={3: 0},
        scratch_shapes=[
            pltpu.SMEM((COLS, 1, DIM), i32),
            pltpu.SMEM((PAIRS,), i32),
            pltpu.VMEM((PARTS, FIRST) + PART, bf16),
            *[pltpu.VMEM((room - FIRST,) + PART, bf16)] * PARTS,
            pltpu.VMEM(HANDED, bf16),
            dma((2,)), dma((PARTS,)),
            dma((PARTS,)), dma((PARTS,)), dma((PARTS, COLS)), dma((PARTS, COLS)),
        ],
        compiler_params=pltpu.CompilerParams(
            collective_id=identity, has_side_effects=True, vmem_limit_bytes=VMEM_BYTES
        ),
        name=f"cross_{room}",
    )


def local(queries, key_value_pages, key_value_scales, page_table, context_len, mig_dest):
    att, got_pages, got_scales, packed, crossed, other, choice = pl.pallas_call(
        first_kernel,
        out_shape=(
            jax.ShapeDtypeStruct(queries.shape, bf16),
            jax.ShapeDtypeStruct(PAGES, bf16),
            jax.ShapeDtypeStruct((NG, 2 * HEADS), bf16),
            jax.ShapeDtypeStruct((PARTS, PAIRS) + PART, bf16),
            jax.ShapeDtypeStruct((PARTS, FIRST) + PART, bf16),
            jax.ShapeDtypeStruct((COLS, 1, DIM), i32),
            jax.ShapeDtypeStruct((1, DIM), i32),
        ),
        in_specs=[hbm] * 6,
        out_specs=(vmem, hbm, vmem, hbm, hbm, vmem, vmem),
        scratch_shapes=[
            pltpu.SMEM(page_table.shape, i32),
            pltpu.SMEM(context_len.shape, i32),
            pltpu.SMEM(mig_dest.shape, i32),
            pltpu.VMEM(queries.shape, bf16),
            pltpu.VMEM((SLOTS, 2 * HEADS), bf16),
            pltpu.VMEM((SLOTS, TOKENS, WIDTH), bf16),
            pltpu.VMEM((COLS, TOKENS, WIDTH), bf16),
            pltpu.VMEM((PARTS, COLS, COLS) + PART, bf16),
            pltpu.VMEM((PARTS, PAIRS) + PART, bf16),
            pltpu.VMEM(HANDED, bf16),
            *[pltpu.VMEM((PAIRS,) + PART, bf16)] * PARTS,
            *[pltpu.VMEM((FIRST,) + PART, bf16)] * PARTS,
            pltpu.VMEM((ROWS, DIM), bf16),
            pltpu.VMEM((NY, NZ, ROWS, DIM), bf16),
            pltpu.VMEM((NY, HEADS + 1, ROWS, DIM), bf16),
            pltpu.VMEM((NY, HEADS + 1, ROWS, DIM), bf16),
            pltpu.VMEM((NZ, 2, ROWS, DIM), bf16),
            pltpu.VMEM((NZ, 2, ROWS, DIM), bf16),
            pltpu.VMEM((2 * HEADS, LOCAL), f32),
            pltpu.VMEM((NG, 1, DIM), f32),
            pltpu.VMEM((NG, 1, DIM), f32),
            pltpu.VMEM((NG, DIM), f32),
            pltpu.VMEM((1, DIM), i32),
            pltpu.VMEM((COLS, 1, DIM), i32),
            pltpu.VMEM((COLS, 1, DIM), i32),
            pltpu.SMEM((COLS, 1, DIM), i32),
            pltpu.SMEM((COLS, 1, DIM), i32),
            pltpu.VMEM((NZ, 1, DIM), f32),
            pltpu.VMEM((NY, 1, DIM), f32),
            pltpu.VMEM((1, DIM), f32),
            pltpu.SMEM((2 * COLS,), i32),
            pltpu.SMEM((2 * COLS,), i32),
            pltpu.SMEM((PAIRS + 1,), i32),
            pltpu.SMEM((PAIRS,), i32),
            pltpu.SMEM((PAIRS,), i32),
            dma((6,)), dma((4 + PARTS,)), dma((PARTS,)),
            dma((NZ,)), dma((NZ,)), dma((NY,)), dma((NY,)),
            dma((PARTS, COLS)), dma((PARTS, COLS)), dma((PARTS,)), dma((PARTS,)),
            dma((COLS,)), dma((COLS,)), dma((PARTS, COLS)), dma((PARTS, COLS)),
            dma((NG,)), dma((NG,)), dma((NG,)), dma((NG,)),
            dma((NY,)), dma((NY,)), dma((NZ,)), dma((NZ,)),
            dma((NZ,)), dma((NZ,)), dma((NY,)), dma((NY,)),
        ],
        compiler_params=pltpu.CompilerParams(
            collective_id=0, has_side_effects=True, vmem_limit_bytes=VMEM_BYTES
        ),
        name="attend_and_migrate",
    )(page_table, context_len, mig_dest, queries, key_value_scales[0], key_value_pages[0])
    got_pages = lax.switch(
        choice[0, 0],
        [lambda packed, crossed, other, pages: pages]
        + [second(room, 1 + i) for i, room in enumerate(ROOM)],
        packed, crossed, other, got_pages,
    )
    return pl.pallas_call(
        last_kernel,
        out_shape=(
            jax.ShapeDtypeStruct(att.shape, bf16),
            jax.ShapeDtypeStruct((1, NG, TOKENS, WIDTH), bf16),
            jax.ShapeDtypeStruct((1,) + got_scales.shape, bf16),
        ),
        in_specs=[hbm] * 3,
        out_specs=(hbm,) * 3,
        scratch_shapes=[
            pltpu.VMEM((NG, TOKENS, WIDTH), bf16),
            pltpu.VMEM(att.shape, bf16),
            pltpu.VMEM(got_scales.shape, bf16),
            dma((CHUNKS + 2,)), dma((CHUNKS + 2,)),
        ],
        compiler_params=pltpu.CompilerParams(vmem_limit_bytes=VMEM_BYTES),
        name="write_results",
    )(att, got_pages.reshape(NG, TOKENS, WIDTH), got_scales)


def solution(mesh):
    return jax.shard_map(
        local,
        mesh=mesh,
        in_specs=(
            P(None, "group", "seq"),
            P("group", "seq", None, None),
            P("group", "seq", None),
            P("group", "seq", None),
            P("group"),
            P("group", "seq"),
        ),
        out_specs=(P(None, "group", "seq"), P("group", "seq", None, None), P("group", "seq", None)),
        check_vma=False,
    )
```

```python
import functools

import jax
import jax.numpy as jnp
from jax import lax
from jax.experimental import pallas as pl
from jax.experimental.pallas import tpu as pltpu
from jax.sharding import PartitionSpec as P

NEGATIVE = -1e30
MESH = pl.DeviceIdType.MESH
NX, NH, NC, NZ, NY = 4, 2, 2, 8, 4
NG = NX * NH * NC
COLS = NX * NC
STEPS, RG, PPR, SLOTS, TOKENS = 4, 2, 8, 16, 32
HEADS, DIM = 8, 128
WIDTH = 2 * HEADS * DIM
LOCAL = SLOTS * TOKENS
ROWS = 16
STRIPE = WIDTH // COLS
PARTS, PART_ROWS, PART_COLS = 4, 16, 128
PAIRS = COLS * COLS
UNROLL = 8
CHUNKS = 8
FIRST = 25
ROOM = (36, PAIRS)


def part_offsets(p):
    return (p // 2) * PART_ROWS, (p % 2) * PART_COLS


def split(value):
    high = value.astype(jnp.bfloat16).astype(jnp.float32)
    middle = (value - high).astype(jnp.bfloat16).astype(jnp.float32)
    return high, middle, value - high - middle


def with_lanes(base, first, spacing, value):
    lane = lax.broadcasted_iota(jnp.int32, base.shape, 1)
    for i, term in enumerate(split(value)):
        base = jnp.where(lane == first + i * spacing, term, base)
    return base


def join(contexts, levels):
    top = jnp.max(levels, axis=0)
    factor = jnp.exp(levels - top[None])
    total = jnp.sum(factor, axis=0)
    context = jnp.sum(contexts.astype(jnp.float32) * factor, axis=0) / total
    return context, jnp.maximum(top + jnp.log(total), NEGATIVE)


def group_of(column, half):
    return ((column // NC) * NH + half) * NC + column % NC


class Place:
    def __init__(self):
        self.g = lax.axis_index("group")
        self.s = lax.axis_index("seq")
        self.x, self.zh, self.c = self.g // (NH * NC), (self.g // NC) % NH, self.g % NC
        self.zl, self.y = self.s // NY, self.s % NY
        self.column = self.x * NC + self.c

    def along_z(self, d):
        return (self.g, lax.rem(self.zl + d, NZ) * NY + self.y)

    def along_y(self, d):
        return (self.g, self.zl * NY + lax.rem(self.y + d, NY))

    def column_at(self, d):
        return lax.rem(self.x + d // NC, NX) * NC + lax.rem(self.c + d % NC, NC)


def remote(src, dst, send_sem, recv_sem, device):
    copy = pltpu.make_async_remote_copy(
        src, dst, send_sem, recv_sem, device_id=device, device_id_type=MESH
    )
    copy.start()
    return copy


def inside(src, dst, sem):
    copy = pltpu.make_async_copy(src, dst, sem)
    copy.start()
    return copy


def wait(copies):
    for copy in copies:
        copy.wait()


def greet(devices):
    barrier = pltpu.get_barrier_semaphore()
    for device in devices:
        pl.semaphore_signal(barrier, 1, device_id=device, device_id_type=MESH)
    return lambda: pl.semaphore_wait(barrier, len(devices))


def repeat(start, stop, step, carry=0):
    def steps(i, carry):
        for k in range(UNROLL):
            carry = step(start + i * UNROLL + k, carry)
        return carry

    rounds = (stop - start) // UNROLL
    carry = lax.fori_loop(0, rounds, steps, carry)
    return lax.fori_loop(start + rounds * UNROLL, stop, step, carry)


def rank_pairs(flags, source_half, dest_half, rank):
    def count_up(pair, before):
        present = flags[pair // COLS, 0, group_of(pair % COLS, dest_half)]
        rank[pair] = jnp.where(present > 0, before, -1)
        return before + present

    repeat(0, PAIRS, count_up, jnp.int32(0))


def hand_over(here, p, handed, out_pages, send_sems, recv_sems, own_sem):
    r0, c0 = part_offsets(p)
    columns = pl.ds(pl.multiple_of(here.column * STRIPE + c0, PART_COLS), PART_COLS)
    target = out_pages.at[:, 1 - here.zh, :, pl.ds(r0, PART_ROWS), columns]
    copies = []
    for d in range(1, COLS):
        i = here.column_at(d)
        copies.append(
            remote(
                handed.at[p, i], target, send_sems.at[p, d], recv_sems.at[p, d],
                (group_of(i, here.zh), here.s),
            )
        )
    copies.append(inside(handed.at[p, here.column], target, own_sem.at[p]))
    return copies


def first_kernel(
    table_in, ctx_in, mig_in, query_in, scales_in, pages_in,
    att_out, out_pages, scales_out, packed_out, crossed_out, other_out, choice_out,
    table, ctx, mig, query, scales, pool, half, stripes, packed, handed,
    relay_0, relay_1, relay_2, relay_3, crossed_0, crossed_1, crossed_2, crossed_3,
    qmine, qall, ypart, yland, zpart, zland, zlevel, zlevel_land, scale_rows, sc_send, sc_recv, sc_all,
    fl_send, fl_same, fl_other, same, other, cz, cy, count,
    slots, found, following, index, rank,
    in_sem, out_sem, own_sem,
    zq_s, zq_r, yq_s, yq_r, st_s, st_r, cr_s, cr_r, ha_s, ha_r, hd_s, hd_r,
    sc_s, sc_r, fl_s, fl_r, yr_s, yr_r, zr_s, zr_r, zv_s, zv_r, cz_s, cz_r, cy_s, cy_r,
):
    relays = (relay_0, relay_1, relay_2, relay_3)
    crossed = (crossed_0, crossed_1, crossed_2, crossed_3)
    here = Place()
    g, s, zh, zl, y, column = here.g, here.s, here.zh, here.zl, here.y, here.column
    get_mig, get_table, get_query, get_pool, get_scales, get_ctx = [
        inside(a, b, in_sem.at[i])
        for i, (a, b) in enumerate(
            [(mig_in, mig), (table_in, table), (query_in, query), (pages_in, pool), (scales_in, scales), (ctx_in, ctx)]
        )
    ]
    same_peers = [(group_of(here.column_at(d), zh), s) for d in range(1, COLS)]
    other_peers = [(group_of(here.column_at(d), 1 - zh), s) for d in range(COLS)]
    z_peers = [here.along_z(d) for d in range(1, NZ)]
    y_peers = [here.along_y(d) for d in range(1, NY)]
    all_here = greet(other_peers + z_peers + same_peers + y_peers)

    get_mig.wait()
    lane = lax.broadcasted_iota(jnp.int32, (1, DIM), 1)
    row_flags = jnp.zeros((1, DIM), jnp.int32)
    for r in range(RG):
        for j in range(PPR):
            row_flags = jnp.where((lane == mig[r, j]) & (lane != g), 1, row_flags)
    fl_send[...] = row_flags
    fl_same[column] = row_flags
    get_table.wait()

    def find_pages(i, carry):
        h = group_of(i % COLS, jnp.where(i < COLS, 1 - zh, zh))
        here_too, slot = jnp.int32(0), jnp.int32(0)
        for r in range(RG):
            for j in range(PPR):
                hit = mig[r, j] == h
                slot = jnp.where(hit, table[0, 0, r * PPR + j], slot)
                here_too = jnp.where(hit, 1, here_too)
        slots[i] = slot
        found[i] = jnp.where(h == g, 0, here_too)
        return carry

    repeat(0, COLS, find_pages)
    get_pool.wait()
    for p in range(PARTS):
        r0, c0 = part_offsets(p)

        def cut_page(b, carry):
            value = pool[slots[b], r0 : r0 + PART_ROWS]
            value = jnp.where(found[b] > 0, value, jnp.zeros_like(value))
            for i in range(COLS):
                start = i * STRIPE + c0
                stripes[p, i, b] = value[:, start : start + PART_COLS]
            return carry

        repeat(0, COLS, cut_page)
        relays[p][pl.ds(column * COLS, COLS)] = stripes[p, column]
    all_here()
    same_flags = [
        remote(fl_send, fl_same.at[column], fl_s.at[d], fl_r.at[d], peer)
        for d, peer in enumerate(same_peers, 1)
    ]
    stripe_copies = []
    for p in range(PARTS):
        place = relays[p].at[pl.ds(column * COLS, COLS)]
        stripe_copies.append(
            [
                remote(stripes.at[p, here.column_at(d)], place, st_s.at[p, d], st_r.at[p, d], peer)
                for d, peer in enumerate(same_peers, 1)
            ]
        )

    other_flags = [
        remote(fl_send, fl_other.at[column], fl_s.at[COLS + d], fl_r.at[COLS + d], peer)
        for d, peer in enumerate(other_peers)
    ]

    get_query.wait()
    mine = query[...].astype(jnp.float32)
    mine = jnp.concatenate(
        [
            mine[t, r : r + 1, hh * DIM : (hh + 1) * DIM]
            for r in range(RG) for hh in range(2) for t in range(STEPS)
        ],
        axis=0,
    ).astype(jnp.bfloat16)
    qmine[...] = mine
    qall[y, zl] = mine
    z_queries = [
        remote(qmine, qall.at[y, zl], zq_s.at[d], zq_r.at[d], peer) for d, peer in enumerate(z_peers, 1)
    ]

    wait(same_flags)
    inside(fl_same, same, out_sem.at[0]).wait()
    following[PAIRS] = PAIRS - 1

    def look_back(i, carry):
        pair = PAIRS - 1 - i
        present = same[pair // COLS, 0, group_of(pair % COLS, 1 - zh)]
        following[pair] = jnp.where(present > 0, pair, following[pair + 1])
        return carry

    repeat(0, PAIRS, look_back)

    def list_pairs(i, cursor):
        pair = following[cursor]
        index[i] = pair
        return jnp.minimum(pair + 1, PAIRS)

    cursor = repeat(0, FIRST, list_pairs, jnp.int32(0))

    def pack(p, start, stop):
        def step(i, carry):
            packed[p, i] = relays[p][index[i]]
            return carry

        repeat(start, stop, step)

    crossings, y_queries, z_counts = [], [], []
    for p in range(PARTS):
        wait(stripe_copies[p])
        pack(p, 0, FIRST)
        crossings.append(
            remote(packed.at[p, pl.ds(0, FIRST)], crossed[p], cr_s.at[p], cr_r.at[p], other_peers[0])
        )
        if p == 0:
            get_scales.wait()
            slot_iota = lax.broadcasted_iota(jnp.int32, (NG, SLOTS), 1)
            dest_iota = lax.broadcasted_iota(jnp.int32, (NG, SLOTS), 0)
            chosen = jnp.zeros((NG, SLOTS), jnp.float32)
            for r in range(RG):
                for j in range(PPR):
                    chosen = jnp.where(
                        (dest_iota == mig[r, j]) & (slot_iota == table[0, 0, r * PPR + j]) & (dest_iota != g),
                        1.0, chosen,
                    )
            own_scales = scales[...]
            rows = jnp.dot(chosen.astype(jnp.bfloat16), own_scales, preferred_element_type=jnp.float32)
            rows = jnp.concatenate([rows, jnp.zeros((NG, DIM - 2 * HEADS), jnp.float32)], axis=1)
            for h in range(NG):
                sc_send[h] = rows[h : h + 1]
            sc_recv[g] = jnp.zeros((1, DIM), jnp.float32)
            scale_copies = [
                remote(sc_send.at[peer[0]], sc_recv.at[g], sc_s.at[d], sc_r.at[d], peer)
                for d, peer in enumerate(other_peers + same_peers)
            ]
            wait(z_queries)
            y_queries = [
                remote(qall.at[y], qall.at[y], yq_s.at[d], yq_r.at[d], peer)
                for d, peer in enumerate(y_peers, 1)
            ]
        if p == 0:
            wait(other_flags)
            source = lax.broadcasted_iota(jnp.int32, (COLS, 1, DIM), 2)
            dest_half = (source // NC) % NH
            per_half = [
                jnp.sum(
                    jnp.sum(jnp.where(dest_half != h, rows[...].astype(jnp.float32), 0.0), axis=0),
                    axis=1, keepdims=True,
                )
                for rows, h in ((fl_same, zh), (fl_other, 1 - zh))
            ]
            count[...] = jnp.broadcast_to(jnp.maximum(per_half[0], per_half[1]), (1, DIM))
            cz[zl] = count[...]
            z_counts = [
                remote(count, cz.at[zl], cz_s.at[d], cz_r.at[d], peer) for d, peer in enumerate(z_peers, 1)
            ]
    other_copy = inside(fl_other, other, out_sem.at[1])

    repeat(COLS, 2 * COLS, find_pages)
    def half_page(b, carry):
        value = pool[slots[COLS + b]]
        half[b] = jnp.where(found[COLS + b] > 0, value, jnp.zeros_like(value))
        return carry

    lax.fori_loop(0, COLS, half_page, 0)
    own_place = out_pages.at[here.x, zh, here.c]
    halves = [
        remote(half.at[here.column_at(d)], own_place, ha_s.at[d], ha_r.at[d], peer)
        for d, peer in enumerate(same_peers, 1)
    ]
    halves.append(inside(half.at[column], own_place, out_sem.at[2]))

    get_ctx.wait()
    token = lax.broadcasted_iota(jnp.int32, (8, LOCAL), 1)
    token_slot, token_in = token // TOKENS, token % TOKENS
    position = jnp.zeros((8, LOCAL), jnp.int32)
    owner = jnp.zeros((8, LOCAL), jnp.int32)
    for r in range(RG):
        for j in range(PPR):
            slot = table[0, 0, r * PPR + j]
            hit = token_slot == slot
            position = jnp.where(hit, (j * NZ * NY + s) * TOKENS + token_in, position)
            owner = jnp.where(hit, r, owner)
    spread = (
        lax.broadcasted_iota(jnp.int32, (SLOTS, LOCAL), 1) // TOKENS
        == lax.broadcasted_iota(jnp.int32, (SLOTS, LOCAL), 0)
    )
    scale_rows[...] = lax.dot_general(
        own_scales, jnp.where(spread, 1.0, 0.0).astype(jnp.bfloat16),
        (((0,), (0,)), ((), ())), preferred_element_type=jnp.float32,
    )
    row = lax.broadcasted_iota(jnp.int32, (NY * ROWS, LOCAL), 0)
    row_request, row_step = (row // 8) % RG, row % STEPS
    limit = jnp.where(row_request == 0, ctx[0], ctx[1]) - STEPS + 1 + row_step
    visible = (position[:1] < limit) & (owner[:1] == row_request)

    wait(y_queries)
    levels = jnp.zeros((NY * ROWS, DIM), jnp.float32)
    for k in range(HEADS):
        query_rows = qall[:, k].reshape(NY * ROWS, DIM)
        keys = pool[:, :, k * DIM : (k + 1) * DIM].reshape(LOCAL, DIM)
        values = pool[:, :, (HEADS + k) * DIM : (HEADS + k + 1) * DIM].reshape(LOCAL, DIM)
        raw = lax.dot_general(
            query_rows, keys, (((1,), (1,)), ((), ())), preferred_element_type=jnp.float32
        )
        scores = raw * (scale_rows[k : k + 1, :] * DIM**-0.5)
        top = jnp.max(jnp.where(visible, scores, NEGATIVE), axis=1, keepdims=True)
        terms = jnp.where(visible, jnp.exp(scores - top), 0.0)
        total = jnp.sum(terms, axis=1, keepdims=True)
        weights = (terms * scale_rows[HEADS + k : HEADS + k + 1, :]).astype(jnp.bfloat16)
        context = jnp.dot(weights, values, preferred_element_type=jnp.float32)
        some = total > 0.0
        total = jnp.where(some, total, 1.0)
        ypart[:, k] = (context / total).astype(jnp.bfloat16).reshape(NY, ROWS, DIM)
        levels = with_lanes(levels, k, HEADS, jnp.where(some, top + jnp.log(total), NEGATIVE))
    ypart[:, HEADS] = levels.astype(jnp.bfloat16).reshape(NY, ROWS, DIM)

    y_parts = [
        remote(ypart.at[lax.rem(y + d, NY)], yland.at[y], yr_s.at[d], yr_r.at[d], peer)
        for d, peer in enumerate(y_peers, 1)
    ]
    yland[y] = ypart[y]

    wait(z_counts)
    count[...] = jnp.max(cz[...], axis=0)
    cy[y] = count[...]
    y_counts = [
        remote(count, cy.at[y], cy_s.at[d], cy_r.at[d], peer) for d, peer in enumerate(y_peers, 1)
    ]

    repeat(FIRST, PAIRS, list_pairs, cursor)
    for p in range(PARTS):
        pack(p, FIRST, PAIRS)
    outs = [inside(packed, packed_out, out_sem.at[3])]

    diagonal = lax.broadcasted_iota(jnp.int32, (ROWS, DIM), 0) == lax.broadcasted_iota(jnp.int32, (ROWS, DIM), 1)
    wait(y_parts)
    terms = yland[:, HEADS].astype(jnp.float32)
    for k in range(HEADS):
        level = sum(terms[:, :, k + i * HEADS : k + i * HEADS + 1] for i in range(3))
        context, level = join(yland[:, k], level)
        zpart[k] = context.astype(jnp.bfloat16)
        zlevel[k] = jnp.sum(jnp.where(diagonal, level, 0.0), axis=0, keepdims=True)
    z_parts = [
        remote(zpart.at[lax.rem(zl + d, NZ)], zland.at[zl], zr_s.at[d], zr_r.at[d], peer)
        for d, peer in enumerate(z_peers, 1)
    ]
    z_parts += [
        remote(zlevel.at[lax.rem(zl + d, NZ)], zlevel_land.at[zl], zv_s.at[d], zv_r.at[d], peer)
        for d, peer in enumerate(z_peers, 1)
    ]
    zland[zl] = zpart[zl]
    zlevel_land[zl] = zlevel[zl]

    other_copy.wait()
    rank_pairs(other, 1 - zh, zh, rank)
    handing = []
    for p in range(PARTS):
        crossings[p].wait()

        def unpack(pair, carry):
            at = rank[pair]
            value = crossed[p][jnp.clip(at, 0, FIRST - 1)]
            value = jnp.where((at >= 0) & (at < FIRST), value, jnp.zeros_like(value))
            handed[p, pair % COLS, pair // COLS // NC, pair // COLS % NC] = value
            return carry

        repeat(0, PAIRS, unpack)
        handing += hand_over(here, p, handed, out_pages, hd_s, hd_r, own_sem)
        outs.append(inside(crossed[p], crossed_out.at[p], out_sem.at[4 + p]))

    wait(z_parts)
    levels = jnp.sum(jnp.where(diagonal[None], zlevel_land[...], 0.0), axis=2, keepdims=True)
    context, _ = join(zland[...], levels)
    for t in range(STEPS):
        att_out[t] = jnp.concatenate(
            [
                jnp.concatenate(
                    [
                        context[r * 8 + hh * STEPS + t : r * 8 + hh * STEPS + t + 1]
                        for hh in range(2)
                    ],
                    axis=1,
                )
                for r in range(RG)
            ],
            axis=0,
        ).astype(jnp.bfloat16)

    wait(scale_copies)
    for h in range(NG):
        sc_all[h : h + 1, :] = sc_recv[h]
    scales_out[...] = sc_all[:, : 2 * HEADS].astype(jnp.bfloat16)
    other_out[...] = fl_other[...]
    wait(y_counts)
    most = jnp.max(cy[...], axis=0)
    choice_out[...] = sum((most > room).astype(jnp.int32) for room in (FIRST,) + ROOM[:-1])
    wait(halves)
    wait(outs)
    wait(handing)


def second_kernel(
    room, packed, first_in, other_in, pages_before,
    out_pages,
    other, rank, first, rest_0, rest_1, rest_2, rest_3, handed, in_sem, own_sem,
    cr_s, cr_r, hd_s, hd_r,
):
    rest = (rest_0, rest_1, rest_2, rest_3)
    here = Place()
    get_other = inside(other_in, other, in_sem.at[0])
    get_first = inside(first_in, first, in_sem.at[1])
    partner = (group_of(here.column, 1 - here.zh), here.s)
    greet([partner] + [(group_of(here.column_at(d), here.zh), here.s) for d in range(1, COLS)])()
    crossings = [
        remote(packed.at[p, pl.ds(FIRST, room - FIRST)], rest[p], cr_s.at[p], cr_r.at[p], partner)
        for p in range(PARTS)
    ]
    get_other.wait()
    rank_pairs(other, 1 - here.zh, here.zh, rank)
    get_first.wait()
    handing = []
    for p in range(PARTS):
        crossings[p].wait()

        def unpack(pair, carry):
            at = rank[pair]
            early = first[p, jnp.clip(at, 0, FIRST - 1)]
            late = rest[p][jnp.clip(at - FIRST, 0, room - FIRST - 1)]
            value = jnp.where(at < FIRST, early, late)
            value = jnp.where(at >= 0, value, jnp.zeros_like(value))
            handed[p, pair % COLS, pair // COLS // NC, pair // COLS % NC] = value
            return carry

        repeat(0, PAIRS, unpack)
        handing += hand_over(here, p, handed, out_pages, hd_s, hd_r, own_sem)
    wait(handing)


def last_kernel(att, pages, scales, att_out, pages_out, scales_out, held, att_held, scales_held, sems, out_sems):
    rows = NG // CHUNKS
    moves = [
        (pages.at[pl.ds(i * rows, rows)], held.at[pl.ds(i * rows, rows)], pages_out.at[0, pl.ds(i * rows, rows)])
        for i in range(CHUNKS)
    ]
    moves += [(att, att_held, att_out), (scales, scales_held, scales_out.at[0])]
    reads = [inside(a, b, sems.at[i]) for i, (a, b, _) in enumerate(moves)]
    writes = []
    for i, (_, b, c) in enumerate(moves):
        reads[i].wait()
        writes.append(inside(b, c, out_sems.at[i]))
    wait(writes)


dma = pltpu.SemaphoreType.DMA
VMEM_BYTES = 63 * 2**20
f32, bf16, i32 = jnp.float32, jnp.bfloat16, jnp.int32
vmem = pl.BlockSpec(memory_space=pltpu.VMEM)
hbm = pl.BlockSpec(memory_space=pltpu.HBM)
PART = (PART_ROWS, PART_COLS)
PAGES = (NX, NH, NC, TOKENS, WIDTH)
HANDED = (PARTS, COLS, NX, NC) + PART


def second(room, identity):
    return pl.pallas_call(
        functools.partial(second_kernel, room),
        out_shape=jax.ShapeDtypeStruct(PAGES, bf16),
        in_specs=[hbm] * 4,
        out_specs=hbm,
        input_output_aliases={3: 0},
        scratch_shapes=[
            pltpu.SMEM((COLS, 1, DIM), i32),
            pltpu.SMEM((PAIRS,), i32),
            pltpu.VMEM((PARTS, FIRST) + PART, bf16),
            *[pltpu.VMEM((room - FIRST,) + PART, bf16)] * PARTS,
            pltpu.VMEM(HANDED, bf16),
            dma((2,)), dma((PARTS,)),
            dma((PARTS,)), dma((PARTS,)), dma((PARTS, COLS)), dma((PARTS, COLS)),
        ],
        compiler_params=pltpu.CompilerParams(
            collective_id=identity, has_side_effects=True, vmem_limit_bytes=VMEM_BYTES
        ),
        name=f"cross_{room}",
    )


def local(queries, key_value_pages, key_value_scales, page_table, context_len, mig_dest):
    att, got_pages, got_scales, packed, crossed, other, choice = pl.pallas_call(
        first_kernel,
        out_shape=(
            jax.ShapeDtypeStruct(queries.shape, bf16),
            jax.ShapeDtypeStruct(PAGES, bf16),
            jax.ShapeDtypeStruct((NG, 2 * HEADS), bf16),
            jax.ShapeDtypeStruct((PARTS, PAIRS) + PART, bf16),
            jax.ShapeDtypeStruct((PARTS, FIRST) + PART, bf16),
            jax.ShapeDtypeStruct((COLS, 1, DIM), i32),
            jax.ShapeDtypeStruct((1, DIM), i32),
        ),
        in_specs=[hbm] * 6,
        out_specs=(vmem, hbm, vmem, hbm, hbm, vmem, vmem),
        scratch_shapes=[
            pltpu.SMEM(page_table.shape, i32),
            pltpu.SMEM(context_len.shape, i32),
            pltpu.SMEM(mig_dest.shape, i32),
            pltpu.VMEM(queries.shape, bf16),
            pltpu.VMEM((SLOTS, 2 * HEADS), bf16),
            pltpu.VMEM((SLOTS, TOKENS, WIDTH), bf16),
            pltpu.VMEM((COLS, TOKENS, WIDTH), bf16),
            pltpu.VMEM((PARTS, COLS, COLS) + PART, bf16),
            pltpu.VMEM((PARTS, PAIRS) + PART, bf16),
            pltpu.VMEM(HANDED, bf16),
            *[pltpu.VMEM((PAIRS,) + PART, bf16)] * PARTS,
            *[pltpu.VMEM((FIRST,) + PART, bf16)] * PARTS,
            pltpu.VMEM((ROWS, DIM), bf16),
            pltpu.VMEM((NY, NZ, ROWS, DIM), bf16),
            pltpu.VMEM((NY, HEADS + 1, ROWS, DIM), bf16),
            pltpu.VMEM((NY, HEADS + 1, ROWS, DIM), bf16),
            pltpu.VMEM((NZ, ROWS, DIM), bf16),
            pltpu.VMEM((NZ, ROWS, DIM), bf16),
            pltpu.VMEM((NZ, 1, DIM), f32),
            pltpu.VMEM((NZ, 1, DIM), f32),
            pltpu.VMEM((2 * HEADS, LOCAL), f32),
            pltpu.VMEM((NG, 1, DIM), f32),
            pltpu.VMEM((NG, 1, DIM), f32),
            pltpu.VMEM((NG, DIM), f32),
            pltpu.VMEM((1, DIM), i32),
            pltpu.VMEM((COLS, 1, DIM), i32),
            pltpu.VMEM((COLS, 1, DIM), i32),
            pltpu.SMEM((COLS, 1, DIM), i32),
            pltpu.SMEM((COLS, 1, DIM), i32),
            pltpu.VMEM((NZ, 1, DIM), f32),
            pltpu.VMEM((NY, 1, DIM), f32),
            pltpu.VMEM((1, DIM), f32),
            pltpu.SMEM((2 * COLS,), i32),
            pltpu.SMEM((2 * COLS,), i32),
            pltpu.SMEM((PAIRS + 1,), i32),
            pltpu.SMEM((PAIRS,), i32),
            pltpu.SMEM((PAIRS,), i32),
            dma((6,)), dma((4 + PARTS,)), dma((PARTS,)),
            dma((NZ,)), dma((NZ,)), dma((NY,)), dma((NY,)),
            dma((PARTS, COLS)), dma((PARTS, COLS)), dma((PARTS,)), dma((PARTS,)),
            dma((COLS,)), dma((COLS,)), dma((PARTS, COLS)), dma((PARTS, COLS)),
            dma((NG,)), dma((NG,)), dma((NG,)), dma((NG,)),
            dma((NY,)), dma((NY,)), dma((NZ,)), dma((NZ,)), dma((NZ,)), dma((NZ,)),
            dma((NZ,)), dma((NZ,)), dma((NY,)), dma((NY,)),
        ],
        compiler_params=pltpu.CompilerParams(
            collective_id=0, has_side_effects=True, vmem_limit_bytes=VMEM_BYTES
        ),
        name="attend_and_migrate",
    )(page_table, context_len, mig_dest, queries, key_value_scales[0], key_value_pages[0])
    got_pages = lax.switch(
        choice[0, 0],
        [lambda packed, crossed, other, pages: pages]
        + [second(room, 1 + i) for i, room in enumerate(ROOM)],
        packed, crossed, other, got_pages,
    )
    return pl.pallas_call(
        last_kernel,
        out_shape=(
            jax.ShapeDtypeStruct(att.shape, bf16),
            jax.ShapeDtypeStruct((1, NG, TOKENS, WIDTH), bf16),
            jax.ShapeDtypeStruct((1,) + got_scales.shape, bf16),
        ),
        in_specs=[hbm] * 3,
        out_specs=(hbm,) * 3,
        scratch_shapes=[
            pltpu.VMEM((NG, TOKENS, WIDTH), bf16),
            pltpu.VMEM(att.shape, bf16),
            pltpu.VMEM(got_scales.shape, bf16),
            dma((CHUNKS + 2,)), dma((CHUNKS + 2,)),
        ],
        compiler_params=pltpu.CompilerParams(vmem_limit_bytes=VMEM_BYTES),
        name="write_results",
    )(att, got_pages.reshape(NG, TOKENS, WIDTH), got_scales)


def solution(mesh):
    return jax.shard_map(
        local,
        mesh=mesh,
        in_specs=(
            P(None, "group", "seq"),
            P("group", "seq", None, None),
            P("group", "seq", None),
            P("group", "seq", None),
            P("group"),
            P("group", "seq"),
        ),
        out_specs=(P(None, "group", "seq"), P("group", "seq", None, None), P("group", "seq", None)),
        check_vma=False,
    )
```
